32 devices in a mesh: dp: 8 (over z, y), tp: 4 (over x, core).
Axes of the slice: x: 2, y: 2, z: 4, core: 2. Of those that a mesh axis runs over, the one named last changes fastest.
Arguments:
- prefill_latent: bfloat16 [1024, 576], P('dp'), may hold values from -5 to 5
- request_slot: int32 [32], replicated, may hold values from 0 to 31, each once
- new_lengths: int32 [8, 4], replicated, may hold values from 1 to 8, 16 in all within a row
- ctx_lengths: int32 [32], P('dp'), may hold values from 1 to 1024, 16384 in all
- kv_cache: bfloat16 [32, 1024, 576], P('dp'), may hold values from -5 to 5
- queries: bfloat16 [2, 32, 128, 576], P(None, 'dp', 'tp'), may hold values from -48 to 48
- step_latents: bfloat16 [2, 32, 576], P(None, 'dp'), may hold values from -5 to 5
- w_uv: bfloat16 [128, 512, 128], P('tp'), may hold values from -0.25 to 0.25
- w_out: bfloat16 [128, 128, 7168], P('tp', None, 'dp'), may hold values from -0.0625 to 0.0625
- hidden: bfloat16 [2, 32, 7168], P(None, None, ('dp', 'tp')), may hold values from -2 to 2
- ffn_gain: float32 [7168], replicated, may hold values from 0.5 to 1.5
- w_gate: bfloat16 [7168, 18432], P(None, ('dp', 'tp')), may hold values from -0.0625 to 0.0625
- w_up: bfloat16 [7168, 18432], P(None, ('dp', 'tp')), may hold values from -0.0625 to 0.0625
- w_down: bfloat16 [18432, 7168], P(('dp', 'tp')), may hold values from -0.078125 to 0.078125
Outputs:
- layer_out: bfloat16 [2, 32, 7168], P(None, None, ('dp', 'tp'))
The draws below stay inside these ranges and needn't reach their ends.
Inputs may be any that keep to these rules, and one draw needn't show every extreme that they name: A permutation of the 32 requests; the owner of request r is request_slot[r] // 4. `new_lengths`: row j lists the 4 requests of owner j; each row sums to 16, and its largest entry is 8. `ctx_lengths`: sums to 16384; the largest is 1024.
All inputs are finite; a program needn't handle non-finite values. No bound on the sum of `ctx_lengths` on one device may be relied on, other than what follows from the above.
Results may differ from the reference program's by a relative error of at most 0.02.
Values may be sent and summed in bfloat16 or wider, within the bound.
A program may use at most 128 MiB of HBM per device.

```python
import math
import jax
import jax.numpy as jnp
import numpy as np
from jax import lax

D = 7168
H = 128
LAT = 512
ROPE = 64
VH = 128
QKD = 192
FF = 18432
RQ = 4
OWN_TOK = 16
CTX_MOST = 1024
STEPS = 2
R = 32
PF_DEV = 128
SEG_MOST = 8
CTX_TOTAL = 16384
N_DP = 8


def latent_pair(key):
    base = jnp.clip(jax.random.normal(jax.random.fold_in(key, 101), (R, CTX_MOST, LAT + ROPE), jnp.float32), -5.0, 5.0)
    return base


def draw_kv_cache(key, part):
    base = latent_pair(key)
    return base.astype(jnp.bfloat16)


def draw_queries(key, part):
    key = jax.random.fold_in(key, 5)
    values = jnp.clip(jax.random.normal(key, (STEPS, R, H, LAT + ROPE), jnp.float32), -5.0, 5.0)
    return values.astype(jnp.bfloat16)


def strengthened(values, rng, source, target, parts, factor):
    def block_of(dim):
        return (jnp.arange(values.shape[dim]) // (values.shape[dim] // parts)).reshape((-1,) + (1,) * (values.ndim - 1 - dim))

    first = jax.random.permutation(rng, parts)[block_of(target)]
    far = (block_of(target) + parts // 2) % parts
    return jnp.where((block_of(source) == first) | (block_of(source) == far), factor * values, values)


def block_levels(stream_key, extent, pieces, smallest, largest):
    factor_of, own = 1.0, jax.random.fold_in(stream_key, 6)
    for dim, blocks in pieces:
        steps = jnp.exp(jax.random.uniform(jax.random.fold_in(own, dim), (blocks,), jnp.float32, smallest / len(pieces), largest / len(pieces)))
        factor_of = factor_of * jnp.repeat(steps, extent[dim] // blocks).reshape([-1 if axis == dim else 1 for axis in range(len(extent))])
    return factor_of


def profile(count, total, reach, skew):
    portions = [(1 << 20) // math.isqrt(standing ** skew) + 1 for standing in range(2, count + 1)]
    rest, holding = total - reach - (count - 1), [1] * (count - 1)
    while rest > 0:
        movable = [i for i in range(count - 1) if holding[i] < reach]
        pool, budget = sum([portions[i] for i in movable]), rest
        for i in movable:
            extra = min(reach - holding[i], max(1, budget * portions[i] // pool), rest)
            holding[i] = holding[i] + extra
            rest = rest - extra
    return np.array([reach] + holding)


def uneven_parts(rng, number_of, total, most, slope):
    if number_of == 2:
        one = jax.random.randint(rng, (), max(1, total - most), min(most, total - 1) + 1)
        return jnp.stack([one, total - one])
    tallies = jnp.asarray(profile(number_of, total, most, slope), jnp.int32)
    couples = (number_of - 1) // 2
    source_of, sink = tallies[1:1 + 2 * couples:2], tallies[2:2 + 2 * couples:2]
    room = jnp.minimum(source_of - 1, most - sink)
    moved = jax.random.randint(jax.random.fold_in(rng, 1), (couples,), 0, 1 << 20) % (room + 1)
    tallies = tallies.at[1:1 + 2 * couples:2].set(source_of - moved).at[2:2 + 2 * couples:2].set(sink + moved)
    return tallies[jax.random.permutation(jax.random.fold_in(rng, 2), number_of)]


def scatter_about(own_key, extent, deviation, limit, split=(), kind=jnp.bfloat16):
    values = deviation * jax.random.normal(own_key, extent, jnp.float32)
    if split:
        values = values * block_levels(own_key, extent, split, -0.22, 0.18)
    return jnp.clip(values, -limit, limit).astype(kind)


def bell_draw_with(key, extent, scale, bound, split, heavy, kind=jnp.bfloat16):
    entries = scale * jax.random.normal(key, extent, jnp.float32)
    if split:
        entries = entries * block_levels(key, extent, split, -0.22, 0.18)
    return jnp.clip(strengthened(entries, jax.random.fold_in(key, 3), *heavy), -bound, bound).astype(kind)


def setup_inputs(seed: int = 0) -> dict:
    seeds = jax.random.split(jax.random.key(seed), 15)
    return {
        "prefill_latent": scatter_about(seeds[0], (N_DP * PF_DEV, LAT + ROPE), 1.0, 5.0, ((0, 8),)),
        "request_slot": jax.random.permutation(seeds[1], R).astype(jnp.int32),
        "new_lengths": jax.vmap(lambda own: uneven_parts(own, RQ, OWN_TOK, OWN_TOK // 2, 1))(jax.random.split(seeds[2], N_DP)).reshape((N_DP, RQ)).astype(jnp.int32),
        "ctx_lengths": uneven_parts(seeds[3], R, CTX_TOTAL, CTX_MOST, 2).astype(jnp.int32),
        "kv_cache": draw_kv_cache(jax.random.fold_in(seeds[14], 71), 0),
        "queries": draw_queries(jax.random.fold_in(seeds[14], 71), 0),
        "step_latents": scatter_about(seeds[6], (STEPS, R, LAT + ROPE), 1.0, 5.0, ((1, 8),)),
        "w_uv": scatter_about(seeds[7], (H, LAT, VH), LAT ** -0.5, 0.25, ((0, 4),)),
        "w_out": bell_draw_with(seeds[8], (H, VH, D), (H * VH) ** -0.5, 0.0625, ((0, 4), (2, 8)), (0, 2, 8, 2.0)),
        "hidden": scatter_about(seeds[9], (STEPS, R, D), 0.3, 2.0, ((2, 32),)),
        "ffn_gain": jnp.clip(1.0 + 0.1 * jax.random.normal(seeds[10], (D,), jnp.float32), 0.5, 1.5),
        "w_gate": scatter_about(seeds[11], (D, FF), D ** -0.5, 0.0625, ((1, 32),)),
        "w_up": scatter_about(seeds[12], (D, FF), D ** -0.5, 0.0625, ((1, 32),)),
        "w_down": bell_draw_with(seeds[13], (FF, D), FF ** -0.5, 0.078125, ((0, 32),), (0, 1, 32, 2.75)),
    }


masked_score = -1e+30
norm_eps = 1e-06

def reference(prefill_latent, request_slot, new_lengths, ctx_lengths, kv_cache, queries, step_latents, w_uv, w_out, hidden, ffn_gain, w_gate, w_up, w_down):
    score_scale = QKD ** (-0.5)
    lengths_flat = new_lengths.reshape(-1)
    request_rows = lengths_flat[request_slot]
    offsets = (jnp.cumsum(request_rows) - request_rows).astype(jnp.int32)
    inverse = jnp.zeros((R,), jnp.int32).at[request_slot].set(jnp.arange(R, dtype=jnp.int32))
    span = jnp.arange(SEG_MOST, dtype=jnp.int32)
    outputs = []
    for step in range(STEPS):

        def attend_one(q_index):
            request = inverse[q_index]
            count = lengths_flat[q_index]
            key_rows = (jnp.arange(N_DP, dtype=jnp.int32)[:, None] * PF_DEV + offsets[request] + span[None, :]).reshape(-1)
            key_rows = jnp.minimum(key_rows, N_DP * PF_DEV - 1).astype(jnp.int32)
            new_keys = prefill_latent[key_rows]
            new_valid = jnp.tile(span < count, N_DP)
            cache_valid = jnp.arange(CTX_MOST, dtype=jnp.int32) < ctx_lengths[q_index]
            all_keys = jnp.concatenate([kv_cache[q_index], new_keys, step_latents[:step + 1, q_index]], axis=0).astype(jnp.float32)
            valid = jnp.concatenate([cache_valid, new_valid, jnp.ones((step + 1,), bool)])
            query = queries[step, q_index].astype(jnp.float32)
            scores = jnp.dot(query, all_keys.T, precision=lax.Precision.HIGHEST, preferred_element_type=jnp.float32) * score_scale
            scores = jnp.where(valid[None, :], scores, masked_score)
            probs = jax.nn.softmax(scores, axis=-1).astype(jnp.bfloat16)
            latent_out = jnp.dot(probs.astype(jnp.float32), all_keys[:, :LAT], precision=lax.Precision.HIGHEST, preferred_element_type=jnp.float32)
            return latent_out.astype(jnp.bfloat16)
        latent_all = lax.map(attend_one, jnp.arange(R, dtype=jnp.int32))
        head_out = jnp.einsum('rhc,hcv->rhv', latent_all.astype(jnp.float32), w_uv.astype(jnp.float32), precision=lax.Precision.HIGHEST).astype(jnp.bfloat16)
        mixed = hidden[step].astype(jnp.float32) + jnp.dot(head_out.reshape(R, H * VH), w_out.reshape(H * VH, D), preferred_element_type=jnp.float32)
        mean_square = lax.optimization_barrier(jnp.mean(mixed * mixed, axis=-1, keepdims=True))
        normed = (mixed * lax.rsqrt(mean_square + norm_eps) * ffn_gain).astype(jnp.bfloat16)
        gate_out = jnp.dot(normed, w_gate, preferred_element_type=jnp.float32)
        up_out = jnp.dot(normed, w_up, preferred_element_type=jnp.float32)
        activated = (jax.nn.silu(gate_out) * up_out).astype(jnp.bfloat16)
        layer_step = mixed + jnp.dot(activated, w_down, preferred_element_type=jnp.float32)
        outputs.append(layer_step.astype(jnp.bfloat16))
    return jnp.stack(outputs, axis=0)
```

```python
import functools

import jax
import jax.numpy as jnp
from jax import lax
from jax.experimental import pallas as pl
from jax.experimental.pallas import tpu as pltpu
from jax.sharding import PartitionSpec as P

LAT = 512
QKD = 192
OWN_TOK = 16


masked_score = -1e30
norm_eps = 1e-06


def attend(query, step_ids, kv_cache, cache_mask, new_rows, new_mask, step_latents, w_uv):
    score_scale = QKD ** (-0.5)
    cache_scores = (
        jnp.einsum("sqhc,qkc->sqhk", query, kv_cache, preferred_element_type=jnp.float32)
        * score_scale
    )
    cache_scores = jnp.where(cache_mask[None, :, None, :], cache_scores, masked_score)
    fresh_scores = (
        jnp.einsum("sqhc,kc->sqhk", query, new_rows, preferred_element_type=jnp.float32)
        * score_scale
    )
    fresh_scores = jnp.where(new_mask[None, :, None, :], fresh_scores, masked_score)
    token_scores = (
        jnp.einsum("sqhc,tqc->sqht", query, step_latents, preferred_element_type=jnp.float32)
        * score_scale
    )
    token_valid = jnp.arange(step_latents.shape[0], dtype=jnp.int32)[None, :] <= step_ids[:, None]
    token_scores = jnp.where(token_valid[:, None, None, :], token_scores, masked_score)
    highest = jnp.maximum(
        jnp.maximum(jnp.max(cache_scores, axis=-1), jnp.max(fresh_scores, axis=-1)),
        jnp.max(token_scores, axis=-1),
    )[..., None]
    cache_exp = jnp.exp(cache_scores - highest)
    fresh_exp = jnp.exp(fresh_scores - highest)
    token_exp = jnp.exp(token_scores - highest)
    totals = (
        jnp.sum(cache_exp, axis=-1, keepdims=True)
        + jnp.sum(fresh_exp, axis=-1, keepdims=True)
        + jnp.sum(token_exp, axis=-1, keepdims=True)
    )
    cache_probs = (cache_exp / totals).astype(jnp.bfloat16)
    fresh_probs = (fresh_exp / totals).astype(jnp.bfloat16)
    token_probs = (token_exp / totals).astype(jnp.bfloat16)
    latent_out = jnp.einsum(
        "sqhk,qkc->sqhc", cache_probs, kv_cache[:, :, :LAT], preferred_element_type=jnp.float32
    )
    latent_out = latent_out + jnp.einsum(
        "sqhk,kc->sqhc", fresh_probs, new_rows[:, :LAT], preferred_element_type=jnp.float32
    )
    latent_out = latent_out + jnp.einsum(
        "sqht,tqc->sqhc", token_probs, step_latents[:, :, :LAT], preferred_element_type=jnp.float32
    )
    latent_out = latent_out.astype(jnp.bfloat16)
    return jnp.einsum(
        "sqhc,hcv->sqhv", latent_out, w_uv, preferred_element_type=jnp.float32
    ).astype(jnp.bfloat16)


def plain_shards(
    prefill_latent,
    request_slot,
    new_lengths,
    ctx_lengths,
    kv_cache,
    queries,
    step_latents,
    w_uv,
    w_out,
    hidden,
    ffn_gain,
    w_gate,
    w_up,
    w_down,
):
    dp_count = lax.axis_size("dp")
    dp_rank = lax.axis_index("dp")
    tp_rank = lax.axis_index("tp")
    per_owner = new_lengths.shape[1]
    total_requests = request_slot.shape[0]
    latent_width = kv_cache.shape[2]
    share_width = hidden.shape[2]
    block_width = w_out.shape[2]
    model_width = block_width * dp_count
    numbers = jnp.arange(total_requests, dtype=jnp.int32)
    one_hot = request_slot[:, None] == numbers[None, :]
    lengths_flat = new_lengths.reshape(-1)
    request_rows = jnp.sum(jnp.where(one_hot, lengths_flat[None, :], 0), axis=1)
    offsets = jnp.cumsum(request_rows) - request_rows
    inverse = jnp.sum(jnp.where(one_hot, numbers[:, None], 0), axis=0)
    slot_start = jnp.cumsum(new_lengths, axis=1) - new_lengths
    positions = jnp.arange(OWN_TOK, dtype=jnp.int32)
    slot_of_place = (
        jnp.sum((slot_start[:, :, None] <= positions[None, None, :]).astype(jnp.int32), axis=1) - 1
    )
    owner_ids = jnp.arange(dp_count, dtype=jnp.int32)[:, None]
    owner_rows = owner_ids * per_owner + slot_of_place
    start_in_slot = jnp.take_along_axis(slot_start, slot_of_place, axis=1)
    source_rows = (
        jnp.take(offsets, jnp.take(inverse, owner_rows)) + positions[None, :] - start_in_slot
    )
    outgoing = jnp.take(prefill_latent, source_rows.reshape(-1), axis=0).reshape(
        dp_count, OWN_TOK, latent_width
    )
    incoming = lax.all_to_all(outgoing, "dp", split_axis=0, concat_axis=0, tiled=True)
    new_rows = incoming.reshape(dp_count * OWN_TOK, latent_width)
    my_lengths = lax.dynamic_index_in_dim(new_lengths, dp_rank, 0, keepdims=False)
    my_start = jnp.cumsum(my_lengths) - my_lengths
    in_slot = (positions[None, :] >= my_start[:, None]) & (
        positions[None, :] < (my_start + my_lengths)[:, None]
    )
    new_mask = jnp.tile(in_slot, (1, dp_count))
    cache_mask = jnp.arange(kv_cache.shape[1], dtype=jnp.int32)[None, :] < ctx_lengths[:, None]
    share_first = tp_rank * share_width

    def finish(first, last):
        step_ids = jnp.arange(first, last, dtype=jnp.int32)
        steps_here = last - first
        head_out = attend(
            queries[first:last],
            step_ids,
            kv_cache,
            cache_mask,
            new_rows,
            new_mask,
            step_latents,
            w_uv,
        )
        every_row = lax.all_gather(head_out, "dp", axis=1, tiled=True)
        partial_value = jnp.dot(
            every_row.reshape(steps_here * total_requests, -1),
            w_out.reshape(-1, block_width),
            preferred_element_type=jnp.float32,
        )
        partial_value = partial_value.reshape(steps_here, total_requests, block_width)
        own_cols = lax.dynamic_slice_in_dim(partial_value, share_first, share_width, 2) + hidden[
            first:last
        ].astype(jnp.float32)
        partial_value = lax.dynamic_update_slice_in_dim(partial_value, own_cols, share_first, 2)
        mixed = lax.psum_scatter(partial_value, "tp", scatter_dimension=2, tiled=True)
        squares = lax.psum(jnp.sum(mixed * mixed, axis=-1), ("dp", "tp"))
        gain_part = lax.dynamic_slice_in_dim(
            ffn_gain, dp_rank * block_width + share_first, share_width
        )
        scaled_part = (mixed * gain_part).astype(jnp.bfloat16)
        scaled = lax.all_gather(scaled_part, ("dp", "tp"), axis=2, tiled=True)
        flat_input = scaled.reshape(steps_here * total_requests, model_width)
        row_scale = lax.rsqrt(squares / model_width + norm_eps).reshape(-1, 1)
        gate_out = jnp.dot(flat_input, w_gate, preferred_element_type=jnp.float32) * row_scale
        up_out = jnp.dot(flat_input, w_up, preferred_element_type=jnp.float32) * row_scale
        activated = (jax.nn.silu(gate_out) * up_out).astype(jnp.bfloat16)
        down_out = jnp.dot(activated, w_down, preferred_element_type=jnp.float32).reshape(
            steps_here, total_requests, model_width
        )
        ffn_part = lax.psum_scatter(down_out, ("dp", "tp"), scatter_dimension=2, tiled=True)
        return (mixed + ffn_part).astype(jnp.bfloat16)

    return finish(0, queries.shape[0])


Z_COUNT, Y_COUNT, X_COUNT, CORES = 4, 2, 2, 2
CHUNKS = 4
PIECE = 256


def dot_f32(left, right):
    return jnp.dot(left, right, preferred_element_type=jnp.float32)


def dot_rows(left, right):
    return lax.dot_general(
        left, right, (((1,), (1,)), ((), ())), preferred_element_type=jnp.float32
    )


def split_pieces(block, share):
    pieces = []
    for index in range(4):
        first = index * share
        base = first // 128 * 128
        last = min(block.shape[1], -(-(first + PIECE) // 128) * 128)
        window = block[:, base:last]
        width = last - base
        if first != base:
            window = pltpu.roll(window, width - (first - base), 1)
        pieces.append(window[:, :PIECE])
    return pieces


def layer_kernel(
    slot_s,
    len_s,
    ctx_s,
    pre_h,
    kv_h,
    qry_h,
    stp_h,
    uv_h,
    wo_h,
    hid_h,
    gain_v,
    wg_h,
    wu_h,
    wd_h,
    out_ref,
    pre,
    kv,
    qry,
    stp,
    uv,
    wo,
    hid,
    wg,
    wu,
    wd,
    tail,
    outg,
    score,
    lat,
    hbuf,
    cpart,
    csend,
    crecv,
    hidf,
    mixed_v,
    xbuf,
    gacc,
    uacc,
    sqacc,
    act,
    e1s,
    e1r,
    keep1,
    e2s,
    e2r,
    keep2,
    e3s,
    e3r,
    e4s,
    e4r,
    load_sem,
    a_send,
    a_recv,
    b_send,
    b_recv,
    c_send,
    c_recv,
    d_send,
    d_recv,
    e1_send,
    e1_recv,
    e2_send,
    e2_recv,
    e3_send,
    e3_recv,
    e4_send,
    e4_recv,
):
    f32, bf16 = jnp.float32, jnp.bfloat16
    dp_count = Z_COUNT * Y_COUNT
    d = lax.axis_index("dp")
    t = lax.axis_index("tp")
    z, y = lax.div(d, Y_COUNT), lax.rem(d, Y_COUNT)
    x, c = lax.div(t, CORES), lax.rem(t, CORES)
    heads = qry.shape[2]
    share = hid.shape[2]
    block_width = 4 * share
    rows = 2 * 4 * dp_count
    y_peer = (z * Y_COUNT + (1 - y), t)
    x_peer = (d, (1 - x) * CORES + c)
    core_peer = (d, x * CORES + (1 - c))

    def z_at(step):
        return lax.rem(z + step, Z_COUNT)

    def send(src, dst, send_sem, recv_sem, device):
        copy = pltpu.make_async_remote_copy(
            src_ref=src,
            dst_ref=dst,
            send_sem=send_sem,
            recv_sem=recv_sem,
            device_id=device,
            device_id_type=pl.DeviceIdType.MESH,
        )
        copy.start()

    def arrived(ref, sem):
        pltpu.make_async_remote_copy(
            src_ref=ref,
            dst_ref=ref,
            send_sem=sem,
            recv_sem=sem,
            device_id=y_peer,
            device_id_type=pl.DeviceIdType.MESH,
        ).wait_recv()

    def sent(ref, sem):
        pltpu.make_async_remote_copy(
            src_ref=ref,
            dst_ref=ref,
            send_sem=sem,
            recv_sem=sem,
            device_id=y_peer,
            device_id_type=pl.DeviceIdType.MESH,
        ).wait_send()

    barrier = pltpu.get_barrier_semaphore()
    for step in range(1, dp_count):
        pl.semaphore_signal(
            barrier,
            inc=1,
            device_id=(lax.rem(d + step, dp_count), t),
            device_id_type=pl.DeviceIdType.MESH,
        )
    for step in range(1, 4):
        pl.semaphore_signal(
            barrier,
            inc=1,
            device_id=(d, lax.rem(t + step, 4)),
            device_id_type=pl.DeviceIdType.MESH,
        )

    def load(index, src, dst):
        copy = pltpu.make_async_copy(src, dst, load_sem.at[index])
        copy.start()
        return copy

    load_pre = load(0, pre_h, pre)
    load_stp = load(1, stp_h, stp)
    load_qry = load(2, qry_h, qry)
    load_kv = [load(3 + i, kv_h.at[i], kv.at[i]) for i in range(4)]
    load_hid = load(7, hid_h, hid)
    load_uv = load(8, uv_h, uv)
    load_wo = load(9, wo_h, wo)
    load_wg = load(10, wg_h, wg)
    load_wu = load(11, wu_h, wu)
    load_wd = load(12, wd_h, wd)

    pf_rows = pre.shape[0]
    source = lax.broadcasted_iota(jnp.int32, (8, pf_rows), 1)

    def place_request(r, carry):
        dest, offset = carry
        owner_row = slot_s[r]
        owner = lax.shift_right_logical(owner_row, 2)
        place = owner_row & 3
        count = len_s[owner, place]
        start = jnp.int32(0)
        for k in range(3):
            start = start + jnp.where(place > k, len_s[owner, k], 0)
        inside = (source >= offset) & (source < offset + count)
        dest = jnp.where(inside, source + (owner * OWN_TOK + start - offset), dest)
        return dest, offset + count

    dest, _ = lax.fori_loop(
        0, 4 * dp_count, place_request, (jnp.full((8, pf_rows), -1, jnp.int32), jnp.int32(0))
    )
    target = lax.broadcasted_iota(jnp.int32, (pf_rows, pf_rows), 0)
    pick = jnp.where(target == dest[0:1], 1.0, 0.0).astype(bf16)
    load_pre.wait()
    outg[...] = dot_f32(pick, pre[...]).astype(bf16)
    pl.semaphore_wait(barrier, dp_count - 1 + 3)

    def own_rows(index):
        return pl.ds(pl.multiple_of(index * OWN_TOK, OWN_TOK), OWN_TOK)

    for step in range(1, dp_count):
        other = lax.rem(d + step, dp_count)
        send(
            outg.at[own_rows(other)],
            tail.at[own_rows(d)],
            a_send.at[step],
            a_recv.at[d],
            (other, t),
        )
    tail[own_rows(d), :] = outg[own_rows(d), :]
    load_stp.wait()
    tokens = jnp.concatenate(
        [
            stp[0].astype(f32),
            stp[1].astype(f32),
            jnp.zeros((tail.shape[0] - pf_rows - 8, stp.shape[2]), f32),
        ],
        axis=0,
    )
    tail[pf_rows:, :] = tokens.astype(bf16)

    load_qry.wait()
    key_block = 256
    for i in range(4):
        load_kv[i].wait()
        query = jnp.concatenate([qry[0, i], qry[1, i]], axis=0)
        for k in range(kv.shape[1] // key_block):
            part = slice(k * key_block, (k + 1) * key_block)
            score[i, :, part] = dot_rows(query, kv[i, part, :])

    load_hid.wait()
    hidf[...] = jnp.zeros_like(hidf)
    hidf[0:32, 0:share] = hid[0].astype(f32)
    hidf[32:64, 0:share] = hid[1].astype(f32)

    for step in range(1, dp_count):
        other = lax.rem(d + step, dp_count)
        arrived(tail.at[own_rows(other)], a_recv.at[other])

    scale = QKD ** (-0.5)
    q_rows = 2 * heads
    tail_col = lax.broadcasted_iota(jnp.int32, (q_rows, tail.shape[0]), 1)
    tail_step = lax.broadcasted_iota(jnp.int32, (q_rows, tail.shape[0]), 0) // heads
    spot = tail_col & (OWN_TOK - 1)
    token = tail_col - pf_rows
    key_col = lax.broadcasted_iota(jnp.int32, (q_rows, kv.shape[1]), 1)
    start = jnp.int32(0)
    for i in range(4):
        count = len_s[d, i]
        query = jnp.concatenate([qry[0, i], qry[1, i]], axis=0)
        tail_score = dot_rows(query, tail[...]) * scale
        fresh_ok = (tail_col < pf_rows) & (spot >= start) & (spot < start + count)
        token_ok = (
            (token >= 0)
            & (token < 8)
            & ((token & 3) == i)
            & (lax.shift_right_arithmetic(token, 2) <= tail_step)
        )
        start = start + count
        tail_score = jnp.where(fresh_ok | token_ok, tail_score, masked_score)
        cache_score = jnp.where(key_col < ctx_s[i], score[i] * scale, masked_score)
        highest = jnp.maximum(
            jnp.max(cache_score, axis=1, keepdims=True), jnp.max(tail_score, axis=1, keepdims=True)
        )
        cache_exp = jnp.exp(cache_score - highest)
        tail_exp = jnp.exp(tail_score - highest)
        total = jnp.sum(cache_exp, axis=1, keepdims=True) + jnp.sum(
            tail_exp, axis=1, keepdims=True
        )
        cache_prob = (cache_exp / total).astype(bf16)
        tail_prob = (tail_exp / total).astype(bf16)
        latent = dot_f32(cache_prob, kv[i, :, :LAT]) + dot_f32(tail_prob, tail[:, :LAT])
        for s in range(2):
            for b in range(LAT // 128):
                lat[b, pl.ds(s * 4 + i, heads, stride=8), :] = latent[
                    s * heads : (s + 1) * heads, b * 128 : (b + 1) * 128
                ]

    half = heads // 2
    per_chunk = half // CHUNKS
    load_uv.wait()

    def head_rows(h):
        return jnp.concatenate(
            [lat[b, h * 8 : (h + 1) * 8, :] for b in range(LAT // 128)], axis=1
        )

    def forward_heads(chunk):
        for step in range(1, Z_COUNT):
            other = z_at(step) * Y_COUNT + y
            arrived(hbuf.at[chunk, other], b_recv.at[chunk, other])
            send(
                hbuf.at[chunk, other],
                hbuf.at[chunk, other],
                b_send.at[chunk, 4 + step],
                b_recv.at[chunk, other],
                y_peer,
            )

    for chunk in range(CHUNKS):
        outs = []
        for p in range(per_chunk):
            h = chunk * per_chunk + p
            both = jnp.concatenate([head_rows(h), head_rows(h + half)], axis=0).astype(bf16)
            low_out = dot_f32(both, uv[h])[0:8]
            high_out = dot_f32(both, uv[h + half])[8:16]
            outs.append(jnp.concatenate([low_out, high_out], axis=0).astype(bf16))
        hbuf[chunk, d] = jnp.concatenate(outs, axis=1)
        for step in range(1, Z_COUNT):
            send(
                hbuf.at[chunk, d],
                hbuf.at[chunk, d],
                b_send.at[chunk, step],
                b_recv.at[chunk, d],
                (z_at(step) * Y_COUNT + y, t),
            )
        send(
            hbuf.at[chunk, d],
            hbuf.at[chunk, d],
            b_send.at[chunk, 0],
            b_recv.at[chunk, d],
            y_peer,
        )
        if chunk >= 1:
            forward_heads(chunk - 1)
    forward_heads(CHUNKS - 1)

    load_wo.wait()
    out_sum = None
    for chunk in range(CHUNKS):
        for step in range(Z_COUNT):
            other = z_at(step) * Y_COUNT + (1 - y)
            arrived(hbuf.at[chunk, other], b_recv.at[chunk, other])
        left = hbuf[chunk].reshape(dp_count * 16, per_chunk * 128)
        for a in range(2):
            first = a * half + chunk * per_chunk
            weight = wo[first : first + per_chunk].reshape(per_chunk * 128, block_width)
            product = dot_f32(left, weight).reshape(dp_count, 16, block_width)
            product = product[:, a * 8 : (a + 1) * 8, :]
            out_sum = product if out_sum is None else out_sum + product
    tiles = []
    for s in range(2):
        for k in range(dp_count // 2):
            tiles.append(out_sum[2 * k, s * 4 : s * 4 + 4])
            tiles.append(out_sum[2 * k + 1, s * 4 : s * 4 + 4])
    partial = jnp.concatenate(tiles, axis=0)
    for index, piece in enumerate(split_pieces(partial, share)):
        cpart[index] = piece
        csend[index] = piece.astype(bf16)
    for step in range(1, 4):
        other = lax.rem(t + step, 4)
        send(csend.at[other], crecv.at[t], c_send.at[step], c_recv.at[t], (d, other))
    mixed = cpart[t] + hidf[...]
    for step in range(1, 4):
        other = lax.rem(t + step, 4)
        arrived(crecv.at[other], c_recv.at[other])
        mixed = mixed + crecv[other].astype(f32)
    lanes = lax.broadcasted_iota(jnp.int32, (rows, PIECE), 1)
    mixed = jnp.where(lanes < share, mixed, 0.0)
    mixed_v[...] = mixed
    squares = jnp.sum(mixed * mixed, axis=1, keepdims=True)
    squares_high = squares.astype(bf16).astype(f32)
    own_block = mixed * gain_v[...]
    own_block = jnp.where(lanes == share, squares_high, own_block)
    own_block = jnp.where(lanes == share + 1, squares - squares_high, own_block)

    def slot_of(cc, xx, yy, zz):
        return ((cc * X_COUNT + xx) * Y_COUNT + yy) * Z_COUNT + zz

    own = slot_of(c, x, y, z)
    xbuf[own] = own_block.astype(bf16)

    def pass_on(slot, kind, number, device):
        send(xbuf.at[slot], xbuf.at[slot], d_send.at[kind, number], d_recv.at[slot], device)

    for step in range(1, Z_COUNT):
        pass_on(own, 0, step, (z_at(step) * Y_COUNT + y, t))
    pass_on(own, 1, 0, y_peer)
    pass_on(own, 2, 0, x_peer)
    pass_on(own, 3, 0, core_peer)

    gacc[...] = jnp.zeros_like(gacc)
    uacc[...] = jnp.zeros_like(uacc)
    sqacc[...] = jnp.zeros_like(sqacc)
    load_wg.wait()
    load_wu.wait()

    def use_block(cc, xx, yy, zz):
        slot = slot_of(cc, xx, yy, zz)
        number = (zz * Y_COUNT + yy) * 4 + xx * CORES + cc
        first = pl.multiple_of(number * share, 32)
        block = xbuf[slot, :, 0:share]
        gacc[...] += dot_f32(block, wg[pl.ds(first, share), :])
        uacc[...] += dot_f32(block, wu[pl.ds(first, share), :])
        sqacc[...] += xbuf[slot, :, 128:256].astype(f32)

    def take(slot):
        arrived(xbuf.at[slot], d_recv.at[slot])

    use_block(c, x, y, z)

    def from_z(step, carry):
        zz = z_at(step)
        slot = slot_of(c, x, y, zz)
        take(slot)
        pass_on(slot, 1, step, y_peer)
        pass_on(slot, 2, step, x_peer)
        pass_on(slot, 3, step, core_peer)
        use_block(c, x, y, zz)
        return carry

    lax.fori_loop(1, Z_COUNT, from_z, 0)

    def from_y(step, carry):
        zz = z_at(step)
        slot = slot_of(c, x, 1 - y, zz)
        take(slot)
        pass_on(slot, 2, 4 + step, x_peer)
        pass_on(slot, 3, 4 + step, core_peer)
        use_block(c, x, 1 - y, zz)
        return carry

    lax.fori_loop(0, Z_COUNT, from_y, 0)

    def from_x(step, carry):
        zz = z_at(step)
        yy = lax.rem(y + lax.div(step, Z_COUNT), 2)
        slot = slot_of(c, 1 - x, yy, zz)
        take(slot)
        pass_on(slot, 3, 8 + step, core_peer)
        use_block(c, 1 - x, yy, zz)
        return carry

    lax.fori_loop(0, 2 * Z_COUNT, from_x, 0)

    def from_core(step, carry):
        zz = z_at(step)
        yy = lax.rem(y + lax.div(step, Z_COUNT), 2)
        xx = lax.rem(x + lax.div(step, 2 * Z_COUNT), 2)
        slot = slot_of(1 - c, xx, yy, zz)
        take(slot)
        use_block(1 - c, xx, yy, zz)
        return carry

    lax.fori_loop(0, 4 * Z_COUNT, from_core, 0)

    sq_lane = lax.broadcasted_iota(jnp.int32, sqacc.shape, 1) + 128
    sq_here = (sq_lane == share) | (sq_lane == share + 1)
    sq_total = jnp.sum(jnp.where(sq_here, sqacc[...], 0.0), axis=1, keepdims=True)
    row_scale = lax.rsqrt(sq_total / (share * 4 * dp_count) + norm_eps)
    gate = gacc[...] * row_scale
    act[...] = (gate / (1.0 + jnp.exp(-gate)) * (uacc[...] * row_scale)).astype(bf16)

    load_wd.wait()

    def dest_dp(i):
        yy = lax.rem(y + 1 + lax.div(i, Z_COUNT), 2)
        return z_at(1 + lax.rem(i, Z_COUNT)) * Y_COUNT + yy

    def over_x(i):
        dd = dest_dp(i)
        arrived(e1r.at[dd], e1_recv.at[dd])
        e2s[dd] = (keep1[dd, 1 - x] + e1r[dd, 1 - x].astype(f32)).astype(bf16)
        send(e2s.at[dd], e2r.at[dd], e2_send.at[dd], e2_recv.at[dd], x_peer)
        keep2[dd] = keep1[dd, x] + e1r[dd, x].astype(f32)

    def down(i, carry):
        dd = dest_dp(i)
        first = pl.multiple_of(dd * block_width, 128)
        product = dot_f32(act[...], wd[:, pl.ds(first, block_width)])
        pieces = split_pieces(product, share)
        for xx in range(X_COUNT):
            zero, one = pieces[2 * xx], pieces[2 * xx + 1]
            keep1[dd, xx] = jnp.where(c == 0, zero, one)
            e1s[dd, xx] = jnp.where(c == 0, one, zero).astype(bf16)
        send(e1s.at[dd], e1r.at[dd], e1_send.at[dd], e1_recv.at[dd], core_peer)

        @pl.when(i >= 2)
        def _():
            over_x(i - 2)

        return carry

    lax.fori_loop(0, dp_count, down, 0)
    over_x(jnp.int32(dp_count - 2))
    over_x(jnp.int32(dp_count - 1))
    for k in range(Z_COUNT):
        zz = z_at(1 + k)
        dd = zz * Y_COUNT + (1 - y)
        arrived(e2r.at[dd], e2_recv.at[dd])
        e3s[zz] = (keep2[dd] + e2r[dd].astype(f32)).astype(bf16)
        send(e3s.at[zz], e3r.at[zz], e3_send.at[zz], e3_recv.at[zz], y_peer)
    result = mixed_v[...]
    for k in range(Z_COUNT):
        zz = z_at(1 + k)
        dd = zz * Y_COUNT + y
        arrived(e2r.at[dd], e2_recv.at[dd])
        arrived(e3r.at[zz], e3_recv.at[zz])
        value = keep2[dd] + e2r[dd].astype(f32) + e3r[zz].astype(f32)
        if k < Z_COUNT - 1:
            e4s[zz] = value.astype(bf16)
            send(e4s.at[zz], e4r.at[z], e4_send.at[zz], e4_recv.at[z], (dd, t))
        else:
            result = result + value
    for step in range(1, Z_COUNT):
        other = z_at(step)
        arrived(e4r.at[other], e4_recv.at[other])
        result = result + e4r[other].astype(f32)
    out_ref[0] = result[0:32, 0:share].astype(bf16)
    out_ref[1] = result[32:64, 0:share].astype(bf16)

    for step in range(1, dp_count):
        sent(outg.at[own_rows(lax.rem(d + step, dp_count))], a_send.at[step])
    for chunk in range(CHUNKS):
        for number in range(8):
            if number != 4:
                sent(hbuf.at[chunk, d], b_send.at[chunk, number])
    for step in range(1, 4):
        sent(csend.at[lax.rem(t + step, 4)], c_send.at[step])
    for kind, numbers in ((0, range(1, 4)), (1, range(4)), (2, range(8)), (3, range(16))):
        for number in numbers:
            sent(xbuf.at[own], d_send.at[kind, number])
    for dd in range(dp_count):
        sent(e1s.at[dd], e1_send.at[dd])
        sent(e2s.at[dd], e2_send.at[dd])
    for zz in range(Z_COUNT):
        sent(e3s.at[zz], e3_send.at[zz])
    for step in range(1, Z_COUNT):
        sent(e4s.at[z_at(step)], e4_send.at[z_at(step)])


def fused_shards(
    prefill_latent,
    request_slot,
    new_lengths,
    ctx_lengths,
    kv_cache,
    queries,
    step_latents,
    w_uv,
    w_out,
    hidden,
    ffn_gain,
    w_gate,
    w_up,
    w_down,
):
    f32, bf16 = jnp.float32, jnp.bfloat16
    share = hidden.shape[2]
    width = kv_cache.shape[2]
    heads = queries.shape[2]
    ff_share = w_gate.shape[1]
    first = (lax.axis_index("dp") * 4 + lax.axis_index("tp")) * share
    gain = lax.dynamic_slice_in_dim(ffn_gain, first, share)
    gain = jnp.pad(gain, (0, PIECE - share)).reshape(1, PIECE)
    smem = pl.BlockSpec(memory_space=pltpu.SMEM)
    vmem = pl.BlockSpec(memory_space=pltpu.VMEM)
    hbm = pl.BlockSpec(memory_space=pl.ANY)
    dma = pltpu.SemaphoreType.DMA
    pieces = (64, PIECE)
    scratch = [
        pltpu.VMEM(prefill_latent.shape, bf16),
        pltpu.VMEM(kv_cache.shape, bf16),
        pltpu.VMEM(queries.shape, bf16),
        pltpu.VMEM(step_latents.shape, bf16),
        pltpu.VMEM(w_uv.shape, bf16),
        pltpu.VMEM(w_out.shape, bf16),
        pltpu.VMEM(hidden.shape, bf16),
        pltpu.VMEM(w_gate.shape, bf16),
        pltpu.VMEM(w_up.shape, bf16),
        pltpu.VMEM(w_down.shape, bf16),
        pltpu.VMEM((prefill_latent.shape[0] + 128, width), bf16),
        pltpu.VMEM(prefill_latent.shape, bf16),
        pltpu.VMEM((4, 2 * heads, kv_cache.shape[1]), f32),
        pltpu.VMEM((LAT // 128, heads * 8, 128), f32),
        pltpu.VMEM((CHUNKS, 8, 16, heads // 2 // CHUNKS * 128), bf16),
        pltpu.VMEM((4, *pieces), f32),
        pltpu.VMEM((4, *pieces), bf16),
        pltpu.VMEM((4, *pieces), bf16),
        pltpu.VMEM(pieces, f32),
        pltpu.VMEM(pieces, f32),
        pltpu.VMEM((32, *pieces), bf16),
        pltpu.VMEM((64, ff_share), f32),
        pltpu.VMEM((64, ff_share), f32),
        pltpu.VMEM((64, 128), f32),
        pltpu.VMEM((64, ff_share), bf16),
        pltpu.VMEM((8, 2, *pieces), bf16),
        pltpu.VMEM((8, 2, *pieces), bf16),
        pltpu.VMEM((8, 2, *pieces), f32),
        pltpu.VMEM((8, *pieces), bf16),
        pltpu.VMEM((8, *pieces), bf16),
        pltpu.VMEM((8, *pieces), f32),
        pltpu.VMEM((4, *pieces), bf16),
        pltpu.VMEM((4, *pieces), bf16),
        pltpu.VMEM((4, *pieces), bf16),
        pltpu.VMEM((4, *pieces), bf16),
        dma((16,)),
        dma((8,)),
        dma((8,)),
        dma((CHUNKS, 8)),
        dma((CHUNKS, 8)),
        dma((4,)),
        dma((4,)),
        dma((4, 16)),
        dma((32,)),
        dma((8,)),
        dma((8,)),
        dma((8,)),
        dma((8,)),
        dma((4,)),
        dma((4,)),
        dma((4,)),
        dma((4,)),
    ]
    return pl.pallas_call(
        layer_kernel,
        out_shape=jax.ShapeDtypeStruct(hidden.shape, bf16),
        in_specs=[smem] * 3 + [hbm] * 7 + [vmem] + [hbm] * 3,
        out_specs=vmem,
        scratch_shapes=scratch,
        compiler_params=pltpu.CompilerParams(
            collective_id=0, has_side_effects=True, vmem_limit_bytes=60 * 1024 * 1024
        ),
        cost_estimate=pl.CostEstimate(
            flops=4_000_000_000, bytes_accessed=42_000_000, transcendentals=400_000
        ),
    )(
        request_slot,
        new_lengths,
        ctx_lengths,
        prefill_latent,
        kv_cache,
        queries,
        step_latents,
        w_uv,
        w_out,
        hidden,
        gain,
        w_gate,
        w_up,
        w_down,
    )


def shards(dp_count, tp_count, *arrays):
    if (dp_count, tp_count) == (Z_COUNT * Y_COUNT, X_COUNT * CORES):
        return fused_shards(*arrays)
    return plain_shards(*arrays)


def solution(mesh):
    return jax.shard_map(
        functools.partial(shards, mesh.shape["dp"], mesh.shape["tp"]),
        mesh=mesh,
        in_specs=(
            P("dp", None),
            P(),
            P(),
            P("dp"),
            P("dp", None, None),
            P(None, "dp", "tp", None),
            P(None, "dp", None),
            P("tp", None, None),
            P("tp", None, "dp"),
            P(None, None, ("dp", "tp")),
            P(),
            P(None, ("dp", "tp")),
            P(None, ("dp", "tp")),
            P(("dp", "tp"), None),
        ),
        out_specs=P(None, None, ("dp", "tp")),
        check_vma=False,
    )
```

```python
import functools

import jax
import jax.numpy as jnp
from jax import lax
from jax.experimental import pallas as pl
from jax.experimental.pallas import tpu as pltpu
from jax.sharding import PartitionSpec as P

LAT = 512
QKD = 192
OWN_TOK = 16


masked_score = -1e30
norm_eps = 1e-06


def attend(query, step_ids, kv_cache, cache_mask, new_rows, new_mask, step_latents, w_uv):
    score_scale = QKD ** (-0.5)
    cache_scores = (
        jnp.einsum("sqhc,qkc->sqhk", query, kv_cache, preferred_element_type=jnp.float32)
        * score_scale
    )
    cache_scores = jnp.where(cache_mask[None, :, None, :], cache_scores, masked_score)
    fresh_scores = (
        jnp.einsum("sqhc,kc->sqhk", query, new_rows, preferred_element_type=jnp.float32)
        * score_scale
    )
    fresh_scores = jnp.where(new_mask[None, :, None, :], fresh_scores, masked_score)
    token_scores = (
        jnp.einsum("sqhc,tqc->sqht", query, step_latents, preferred_element_type=jnp.float32)
        * score_scale
    )
    token_valid = jnp.arange(step_latents.shape[0], dtype=jnp.int32)[None, :] <= step_ids[:, None]
    token_scores = jnp.where(token_valid[:, None, None, :], token_scores, masked_score)
    highest = jnp.maximum(
        jnp.maximum(jnp.max(cache_scores, axis=-1), jnp.max(fresh_scores, axis=-1)),
        jnp.max(token_scores, axis=-1),
    )[..., None]
    cache_exp = jnp.exp(cache_scores - highest)
    fresh_exp = jnp.exp(fresh_scores - highest)
    token_exp = jnp.exp(token_scores - highest)
    totals = (
        jnp.sum(cache_exp, axis=-1, keepdims=True)
        + jnp.sum(fresh_exp, axis=-1, keepdims=True)
        + jnp.sum(token_exp, axis=-1, keepdims=True)
    )
    cache_probs = (cache_exp / totals).astype(jnp.bfloat16)
    fresh_probs = (fresh_exp / totals).astype(jnp.bfloat16)
    token_probs = (token_exp / totals).astype(jnp.bfloat16)
    latent_out = jnp.einsum(
        "sqhk,qkc->sqhc", cache_probs, kv_cache[:, :, :LAT], preferred_element_type=jnp.float32
    )
    latent_out = latent_out + jnp.einsum(
        "sqhk,kc->sqhc", fresh_probs, new_rows[:, :LAT], preferred_element_type=jnp.float32
    )
    latent_out = latent_out + jnp.einsum(
        "sqht,tqc->sqhc", token_probs, step_latents[:, :, :LAT], preferred_element_type=jnp.float32
    )
    latent_out = latent_out.astype(jnp.bfloat16)
    return jnp.einsum(
        "sqhc,hcv->sqhv", latent_out, w_uv, preferred_element_type=jnp.float32
    ).astype(jnp.bfloat16)


def plain_shards(
    prefill_latent,
    request_slot,
    new_lengths,
    ctx_lengths,
    kv_cache,
    queries,
    step_latents,
    w_uv,
    w_out,
    hidden,
    ffn_gain,
    w_gate,
    w_up,
    w_down,
):
    dp_count = lax.axis_size("dp")
    dp_rank = lax.axis_index("dp")
    tp_rank = lax.axis_index("tp")
    per_owner = new_lengths.shape[1]
    total_requests = request_slot.shape[0]
    latent_width = kv_cache.shape[2]
    share_width = hidden.shape[2]
    block_width = w_out.shape[2]
    model_width = block_width * dp_count
    numbers = jnp.arange(total_requests, dtype=jnp.int32)
    one_hot = request_slot[:, None] == numbers[None, :]
    lengths_flat = new_lengths.reshape(-1)
    request_rows = jnp.sum(jnp.where(one_hot, lengths_flat[None, :], 0), axis=1)
    offsets = jnp.cumsum(request_rows) - request_rows
    inverse = jnp.sum(jnp.where(one_hot, numbers[:, None], 0), axis=0)
    slot_start = jnp.cumsum(new_lengths, axis=1) - new_lengths
    positions = jnp.arange(OWN_TOK, dtype=jnp.int32)
    slot_of_place = (
        jnp.sum((slot_start[:, :, None] <= positions[None, None, :]).astype(jnp.int32), axis=1) - 1
    )
    owner_ids = jnp.arange(dp_count, dtype=jnp.int32)[:, None]
    owner_rows = owner_ids * per_owner + slot_of_place
    start_in_slot = jnp.take_along_axis(slot_start, slot_of_place, axis=1)
    source_rows = (
        jnp.take(offsets, jnp.take(inverse, owner_rows)) + positions[None, :] - start_in_slot
    )
    outgoing = jnp.take(prefill_latent, source_rows.reshape(-1), axis=0).reshape(
        dp_count, OWN_TOK, latent_width
    )
    incoming = lax.all_to_all(outgoing, "dp", split_axis=0, concat_axis=0, tiled=True)
    new_rows = incoming.reshape(dp_count * OWN_TOK, latent_width)
    my_lengths = lax.dynamic_index_in_dim(new_lengths, dp_rank, 0, keepdims=False)
    my_start = jnp.cumsum(my_lengths) - my_lengths
    in_slot = (positions[None, :] >= my_start[:, None]) & (
        positions[None, :] < (my_start + my_lengths)[:, None]
    )
    new_mask = jnp.tile(in_slot, (1, dp_count))
    cache_mask = jnp.arange(kv_cache.shape[1], dtype=jnp.int32)[None, :] < ctx_lengths[:, None]
    share_first = tp_rank * share_width

    def finish(first, last):
        step_ids = jnp.arange(first, last, dtype=jnp.int32)
        steps_here = last - first
        head_out = attend(
            queries[first:last],
            step_ids,
            kv_cache,
            cache_mask,
            new_rows,
            new_mask,
            step_latents,
            w_uv,
        )
        every_row = lax.all_gather(head_out, "dp", axis=1, tiled=True)
        partial_value = jnp.dot(
            every_row.reshape(steps_here * total_requests, -1),
            w_out.reshape(-1, block_width),
            preferred_element_type=jnp.float32,
        )
        partial_value = partial_value.reshape(steps_here, total_requests, block_width)
        own_cols = lax.dynamic_slice_in_dim(partial_value, share_first, share_width, 2) + hidden[
            first:last
        ].astype(jnp.float32)
        partial_value = lax.dynamic_update_slice_in_dim(partial_value, own_cols, share_first, 2)
        mixed = lax.psum_scatter(partial_value, "tp", scatter_dimension=2, tiled=True)
        squares = lax.psum(jnp.sum(mixed * mixed, axis=-1), ("dp", "tp"))
        gain_part = lax.dynamic_slice_in_dim(
            ffn_gain, dp_rank * block_width + share_first, share_width
        )
        scaled_part = (mixed * gain_part).astype(jnp.bfloat16)
        scaled = lax.all_gather(scaled_part, ("dp", "tp"), axis=2, tiled=True)
        flat_input = scaled.reshape(steps_here * total_requests, model_width)
        row_scale = lax.rsqrt(squares / model_width + norm_eps).reshape(-1, 1)
        gate_out = jnp.dot(flat_input, w_gate, preferred_element_type=jnp.float32) * row_scale
        up_out = jnp.dot(flat_input, w_up, preferred_element_type=jnp.float32) * row_scale
        activated = (jax.nn.silu(gate_out) * up_out).astype(jnp.bfloat16)
        down_out = jnp.dot(activated, w_down, preferred_element_type=jnp.float32).reshape(
            steps_here, total_requests, model_width
        )
        ffn_part = lax.psum_scatter(down_out, ("dp", "tp"), scatter_dimension=2, tiled=True)
        return (mixed + ffn_part).astype(jnp.bfloat16)

    return finish(0, queries.shape[0])


Z_COUNT, Y_COUNT, X_COUNT, CORES = 4, 2, 2, 2
CHUNKS = 4
WINDOW = 512


def dot_f32(left, right):
    return jnp.dot(left, right, preferred_element_type=jnp.float32)


def dot_rows(left, right):
    return lax.dot_general(
        left, right, (((1,), (1,)), ((), ())), preferred_element_type=jnp.float32
    )


def layer_kernel(
    slot_s,
    len_s,
    ctx_s,
    pre_h,
    kv_h,
    qry_h,
    stp_h,
    uv_h,
    wo_h,
    hid_h,
    gain_v,
    wg_h,
    wu_h,
    wd_h,
    out_ref,
    pre,
    kv,
    qry,
    stp,
    uv,
    wo,
    hid,
    wg,
    wu,
    wd,
    tail,
    outg,
    score,
    lat,
    hbuf,
    cpart,
    csend,
    crecv,
    hidw,
    mixed_v,
    xbuf,
    gacc,
    uacc,
    sqacc,
    act,
    e1s,
    e1r,
    keep1,
    e2s,
    e2r,
    keep2,
    e3s,
    e3r,
    e4s,
    e4r,
    fsend,
    frecv,
    load_sem,
    a_send,
    a_recv,
    b_send,
    b_recv,
    c_send,
    c_recv,
    d_send,
    d_recv,
    e1_send,
    e1_recv,
    e2_send,
    e2_recv,
    e3_send,
    e3_recv,
    e4_send,
    e4_recv,
    f_send,
    f_recv,
):
    f32, bf16 = jnp.float32, jnp.bfloat16
    dp_count = Z_COUNT * Y_COUNT
    d = lax.axis_index("dp")
    t = lax.axis_index("tp")
    z, y = lax.div(d, Y_COUNT), lax.rem(d, Y_COUNT)
    x, c = lax.div(t, CORES), lax.rem(t, CORES)
    heads = qry.shape[2]
    share = hid.shape[2]
    block_width = 4 * share
    rows = 2 * 4 * dp_count
    y_peer = (z * Y_COUNT + (1 - y), t)
    x_peer = (d, (1 - x) * CORES + c)
    core_peer = (d, x * CORES + (1 - c))

    def z_at(step):
        return lax.rem(z + step, Z_COUNT)

    def send(src, dst, send_sem, recv_sem, device):
        copy = pltpu.make_async_remote_copy(
            src_ref=src,
            dst_ref=dst,
            send_sem=send_sem,
            recv_sem=recv_sem,
            device_id=device,
            device_id_type=pl.DeviceIdType.MESH,
        )
        copy.start()

    def arrived(ref, sem):
        pltpu.make_async_remote_copy(
            src_ref=ref,
            dst_ref=ref,
            send_sem=sem,
            recv_sem=sem,
            device_id=y_peer,
            device_id_type=pl.DeviceIdType.MESH,
        ).wait_recv()

    def sent(ref, sem):
        pltpu.make_async_remote_copy(
            src_ref=ref,
            dst_ref=ref,
            send_sem=sem,
            recv_sem=sem,
            device_id=y_peer,
            device_id_type=pl.DeviceIdType.MESH,
        ).wait_send()

    barrier = pltpu.get_barrier_semaphore()
    for step in range(1, dp_count):
        pl.semaphore_signal(
            barrier,
            inc=1,
            device_id=(lax.rem(d + step, dp_count), t),
            device_id_type=pl.DeviceIdType.MESH,
        )
    for step in range(1, 4):
        pl.semaphore_signal(
            barrier,
            inc=1,
            device_id=(d, lax.rem(t + step, 4)),
            device_id_type=pl.DeviceIdType.MESH,
        )

    def load(index, src, dst):
        copy = pltpu.make_async_copy(src, dst, load_sem.at[index])
        copy.start()
        return copy

    load_pre = load(0, pre_h, pre)
    load_stp = load(1, stp_h, stp)
    load_qry = load(2, qry_h, qry)
    load_kv = [load(3 + i, kv_h.at[i], kv.at[i]) for i in range(4)]
    load_hid = load(7, hid_h, hid)
    load_uv = load(8, uv_h, uv)

    pf_rows = pre.shape[1]
    source = lax.broadcasted_iota(jnp.int32, (8, pf_rows), 1)

    def place_request(r, carry):
        dest, offset = carry
        owner_row = slot_s[r]
        owner = lax.shift_right_logical(owner_row, 2)
        place = owner_row & 3
        count = len_s[place, owner]
        start = jnp.int32(0)
        for k in range(3):
            start = start + jnp.where(place > k, len_s[k, owner], 0)
        inside = (source >= offset) & (source < offset + count)
        dest = jnp.where(inside, source + (owner * OWN_TOK + start - offset), dest)
        return dest, offset + count

    dest, _ = lax.fori_loop(
        0, 4 * dp_count, place_request, (jnp.full((8, pf_rows), -1, jnp.int32), jnp.int32(0))
    )
    target = lax.broadcasted_iota(jnp.int32, (pf_rows, pf_rows), 0)
    pick = jnp.where(target == dest[0:1], 1.0, 0.0).astype(bf16)
    load_pre.wait()
    outg[...] = dot_rows(pick, pre[...]).astype(bf16)
    pl.semaphore_wait(barrier, dp_count - 1 + 3)

    def own_rows(index):
        return pl.ds(pl.multiple_of(index * OWN_TOK, OWN_TOK), OWN_TOK)

    for step in range(1, dp_count):
        other = lax.rem(d + step, dp_count)
        send(
            outg.at[own_rows(other)],
            tail.at[own_rows(d)],
            a_send.at[step],
            a_recv.at[d],
            (other, t),
        )
    tail[own_rows(d), :] = outg[own_rows(d), :]
    load_stp.wait()
    tokens = jnp.concatenate(
        [
            stp[0].astype(f32),
            stp[1].astype(f32),
            jnp.zeros((tail.shape[0] - pf_rows - 8, stp.shape[2]), f32),
        ],
        axis=0,
    )
    tail[pf_rows:, :] = tokens.astype(bf16)

    load_qry.wait()
    key_block = 256
    for i in range(4):
        load_kv[i].wait()
        query = jnp.concatenate([qry[0, i], qry[1, i]], axis=0)
        for k in range(kv.shape[2] // key_block):
            part = slice(k * key_block, (k + 1) * key_block)
            score[i, :, part] = dot_f32(query, kv[i, :, part])
        if i == 1:
            load_wo = load(9, wo_h, wo)
    load_wg = load(10, wg_h, wg)
    load_wu = load(11, wu_h, wu)
    load_wd = load(12, wd_h, wd)

    load_hid.wait()
    hidw[...] = jnp.zeros_like(hidw)
    for s in range(2):
        hidw[s, :, 0:share] = hid[s].astype(f32)
    for s in range(2):
        narrow = hidw[s]
        placed = narrow
        for k in range(1, 4):
            placed = jnp.where(t == k, pltpu.roll(narrow, k * share, 1), placed)
        hidw[s] = placed

    for step in range(1, dp_count):
        other = lax.rem(d + step, dp_count)
        arrived(tail.at[own_rows(other)], a_recv.at[other])

    scale = QKD ** (-0.5)
    q_rows = 2 * heads
    tail_col = lax.broadcasted_iota(jnp.int32, (q_rows, tail.shape[0]), 1)
    tail_step = lax.broadcasted_iota(jnp.int32, (q_rows, tail.shape[0]), 0) // heads
    spot = tail_col & (OWN_TOK - 1)
    token = tail_col - pf_rows
    key_col = lax.broadcasted_iota(jnp.int32, (q_rows, kv.shape[2]), 1)
    start = jnp.int32(0)
    for i in range(4):
        count = len_s[i, d]
        query = jnp.concatenate([qry[0, i], qry[1, i]], axis=0)
        tail_score = dot_rows(query, tail[...]) * scale
        fresh_ok = (tail_col < pf_rows) & (spot >= start) & (spot < start + count)
        token_ok = (
            (token >= 0)
            & (token < 8)
            & ((token & 3) == i)
            & (lax.shift_right_arithmetic(token, 2) <= tail_step)
        )
        start = start + count
        tail_score = jnp.where(fresh_ok | token_ok, tail_score, masked_score)
        cache_score = jnp.where(key_col < ctx_s[i], score[i] * scale, masked_score)
        highest = jnp.maximum(
            jnp.max(cache_score, axis=1, keepdims=True), jnp.max(tail_score, axis=1, keepdims=True)
        )
        cache_exp = jnp.exp(cache_score - highest)
        tail_exp = jnp.exp(tail_score - highest)
        total = jnp.sum(cache_exp, axis=1, keepdims=True) + jnp.sum(
            tail_exp, axis=1, keepdims=True
        )
        cache_prob = (cache_exp / total).astype(bf16)
        tail_prob = (tail_exp / total).astype(bf16)
        cache_part = dot_rows(kv[i, 0:LAT, :], cache_prob)
        latent = jnp.transpose(cache_part) + dot_f32(tail_prob, tail[:, :LAT])
        for s in range(2):
            for b in range(LAT // 128):
                lat[b, pl.ds(s * 4 + i, heads, stride=8), :] = latent[
                    s * heads : (s + 1) * heads, b * 128 : (b + 1) * 128
                ]

    half = heads // 2
    per_chunk = half // CHUNKS
    load_uv.wait()

    def head_rows(h):
        return jnp.concatenate(
            [lat[b, h * 8 : (h + 1) * 8, :] for b in range(LAT // 128)], axis=1
        )

    def forward_heads(chunk):
        for step in range(1, Z_COUNT):
            other = z_at(step) * Y_COUNT + y
            arrived(hbuf.at[chunk, other], b_recv.at[chunk, other])
            send(
                hbuf.at[chunk, other],
                hbuf.at[chunk, other],
                b_send.at[chunk, 4 + step],
                b_recv.at[chunk, other],
                y_peer,
            )

    for chunk in range(CHUNKS):
        outs = []
        for p in range(per_chunk):
            h = chunk * per_chunk + p
            both = jnp.concatenate([head_rows(h), head_rows(h + half)], axis=0).astype(bf16)
            low_out = dot_f32(both, uv[h])[0:8]
            high_out = dot_f32(both, uv[h + half])[8:16]
            outs.append(jnp.concatenate([low_out, high_out], axis=0).astype(bf16))
        hbuf[chunk, d] = jnp.concatenate(outs, axis=1)
        for step in range(1, Z_COUNT):
            send(
                hbuf.at[chunk, d],
                hbuf.at[chunk, d],
                b_send.at[chunk, step],
                b_recv.at[chunk, d],
                (z_at(step) * Y_COUNT + y, t),
            )
        send(
            hbuf.at[chunk, d],
            hbuf.at[chunk, d],
            b_send.at[chunk, 0],
            b_recv.at[chunk, d],
            y_peer,
        )
        if chunk >= 1:
            forward_heads(chunk - 1)
    forward_heads(CHUNKS - 1)

    load_wo.wait()
    out_sum = None
    for chunk in range(CHUNKS):
        for step in range(Z_COUNT):
            other = z_at(step) * Y_COUNT + (1 - y)
            arrived(hbuf.at[chunk, other], b_recv.at[chunk, other])
        left = hbuf[chunk].reshape(dp_count * 16, per_chunk * 128)
        for a in range(2):
            first = a * half + chunk * per_chunk
            weight = wo[first : first + per_chunk].reshape(per_chunk * 128, block_width)
            product = dot_f32(left, weight).reshape(dp_count, 16, block_width)
            product = product[:, a * 8 : (a + 1) * 8, :]
            out_sum = product if out_sum is None else out_sum + product
    partial = []
    for s in range(2):
        tiles = []
        for k in range(dp_count):
            tiles.append(out_sum[k, s * 4 : s * 4 + 4])
        partial.append(jnp.concatenate(tiles, axis=0) + hidw[s])
    for xx in range(X_COUNT):
        for cc in range(CORES):
            piece = partial[cc][:, xx * 384 : xx * 384 + WINDOW]
            cpart[xx * CORES + cc] = piece
            csend[xx * CORES + cc] = piece.astype(bf16)
    for step in range(1, 4):
        other = lax.rem(t + step, 4)
        send(csend.at[other], crecv.at[t], c_send.at[step], c_recv.at[t], (d, other))
    gain = jnp.concatenate(
        [gain_v[pl.ds(d * (block_width // 128) + x * 3 + k, 1), :] for k in range(4)], axis=1
    )
    mixed = cpart[t]
    for step in range(1, 4):
        other = lax.rem(t + step, 4)
        arrived(crecv.at[other], c_recv.at[other])
        mixed = mixed + crecv[other].astype(f32)
    lanes = lax.broadcasted_iota(jnp.int32, mixed.shape, 1)
    pair = 2 * share
    mixed = jnp.where((lanes >= 64 * x) & (lanes < 64 * x + pair), mixed, 0.0)
    mixed_v[...] = mixed
    squares = jnp.sum(mixed * mixed, axis=1, keepdims=True)
    squares_high = squares.astype(bf16).astype(f32)
    spare = pair * (1 - x)
    own_block = mixed * gain
    own_block = jnp.where(lanes == spare, squares_high, own_block)
    own_block = jnp.where(lanes == spare + 1, squares - squares_high, own_block)

    def place_of(n):
        xx = lax.rem(x + lax.div(n, 2 * Z_COUNT), 2)
        yy = lax.rem(y + lax.rem(lax.div(n, Z_COUNT), 2), 2)
        return xx, yy, z_at(lax.rem(n, Z_COUNT))

    def slot_of(n):
        xx, yy, zz = place_of(n)
        return (xx * Y_COUNT + yy) * Z_COUNT + zz

    own = slot_of(jnp.int32(0))
    xbuf[own, c] = own_block.astype(bf16)

    def pass_on(slot, kind, number, device):
        send(
            xbuf.at[slot, c],
            xbuf.at[slot, c],
            d_send.at[kind, number],
            d_recv.at[slot * 2 + c],
            device,
        )

    for step in range(1, Z_COUNT):
        pass_on(own, 0, step, (z_at(step) * Y_COUNT + y, t))
    pass_on(own, 1, 0, y_peer)
    pass_on(own, 2, 0, x_peer)
    pass_on(own, 3, 0, core_peer)

    gacc[...] = jnp.zeros_like(gacc)
    uacc[...] = jnp.zeros_like(uacc)
    sqacc[...] = jnp.zeros_like(sqacc)
    load_wg.wait()
    load_wu.wait()
    block_lane = lax.broadcasted_iota(jnp.int32, (rows, WINDOW), 1)

    def use_block(n):
        xx, yy, zz = place_of(n)
        slot = (xx * Y_COUNT + yy) * Z_COUNT + zz
        arrived(xbuf.at[slot, 1 - c], d_recv.at[slot * 2 + (1 - c)])
        block = xbuf[slot].reshape(rows, WINDOW).astype(f32)
        inside = (block_lane >= 64 * xx) & (block_lane < 64 * xx + pair)
        block = jnp.where(inside, block, 0.0).astype(bf16)
        first = pl.multiple_of((zz * Y_COUNT + yy) * block_width + xx * 384, 128)
        gacc[...] += dot_rows(wg[:, pl.ds(first, WINDOW)], block)
        uacc[...] += dot_rows(wu[:, pl.ds(first, WINDOW)], block)
        lane = pl.multiple_of(384 * (1 - xx), 128)
        sqacc[xx] += xbuf[slot, :, :, pl.ds(lane, 128)].reshape(rows, 128).astype(f32)

    def take(n):
        slot = slot_of(n)
        arrived(xbuf.at[slot, c], d_recv.at[slot * 2 + c])
        return slot

    def from_z(n, carry):
        slot = take(n)
        pass_on(slot, 1, n, y_peer)
        pass_on(slot, 2, n, x_peer)
        pass_on(slot, 3, n, core_peer)
        return carry

    def from_y(n, carry):
        slot = take(n)
        pass_on(slot, 2, n, x_peer)
        pass_on(slot, 3, n, core_peer)
        use_block(n - 3)
        return carry

    def from_x(n, carry):
        slot = take(n)
        pass_on(slot, 3, n, core_peer)
        use_block(n - 3)
        return carry

    def last(n, carry):
        use_block(n)
        return carry

    use_block(jnp.int32(0))
    lax.fori_loop(1, Z_COUNT, from_z, 0)
    lax.fori_loop(Z_COUNT, 2 * Z_COUNT, from_y, 0)
    lax.fori_loop(2 * Z_COUNT, 4 * Z_COUNT, from_x, 0)
    lax.fori_loop(4 * Z_COUNT - 3, 4 * Z_COUNT, last, 0)

    sq_lane = lax.broadcasted_iota(jnp.int32, (rows, 128), 1)
    sq_all = jnp.where((sq_lane == pair - 384) | (sq_lane == pair - 383), sqacc[0], 0.0)
    sq_all = sq_all + jnp.where(sq_lane < 2, sqacc[1], 0.0)
    sq_total = jnp.sum(jnp.transpose(sq_all), axis=0, keepdims=True)
    token_scale = lax.rsqrt(sq_total / (block_width * dp_count) + norm_eps)
    gate = gacc[...] * token_scale
    hidden_units = gate / (1.0 + jnp.exp(-gate)) * (uacc[...] * token_scale)
    by_token = jnp.transpose(hidden_units)
    act[0:32] = jnp.where(c == 0, by_token[0:32], by_token[32:64]).astype(bf16)
    act[32:64] = jnp.where(c == 0, by_token[32:64], by_token[0:32]).astype(bf16)

    load_wd.wait()

    def dest_dp(i):
        yy = lax.rem(y + 1 + lax.div(i, Z_COUNT), 2)
        return z_at(1 + lax.rem(i, Z_COUNT)) * Y_COUNT + yy

    def over_x(i):
        dd = dest_dp(i)
        arrived(e1r.at[dd], e1_recv.at[dd])
        e2s[dd] = (keep1[dd, 1 - x] + e1r[dd, 1 - x].astype(f32)).astype(bf16)
        send(e2s.at[dd], e2r.at[dd], e2_send.at[dd], e2_recv.at[dd], x_peer)
        keep2[dd] = keep1[dd, x] + e1r[dd, x].astype(f32)

    def down(i, carry):
        dd = dest_dp(i)
        first = pl.multiple_of(dd * block_width, 128)
        product = dot_f32(act[...], wd[:, pl.ds(first, block_width)])
        for xx in range(X_COUNT):
            window = slice(xx * 384, xx * 384 + WINDOW)
            keep1[dd, xx] = product[0:32, window]
            e1s[dd, xx] = product[32:64, window].astype(bf16)
        send(e1s.at[dd], e1r.at[dd], e1_send.at[dd], e1_recv.at[dd], core_peer)

        @pl.when(i >= 2)
        def _():
            over_x(i - 2)

        return carry

    lax.fori_loop(0, dp_count, down, 0)
    over_x(jnp.int32(dp_count - 2))
    over_x(jnp.int32(dp_count - 1))
    for k in range(Z_COUNT):
        zz = z_at(1 + k)
        dd = zz * Y_COUNT + (1 - y)
        arrived(e2r.at[dd], e2_recv.at[dd])
        e3s[zz] = (keep2[dd] + e2r[dd].astype(f32)).astype(bf16)
        send(e3s.at[zz], e3r.at[zz], e3_send.at[zz], e3_recv.at[zz], y_peer)
    result = mixed_v[...]
    for k in range(Z_COUNT):
        zz = z_at(1 + k)
        dd = zz * Y_COUNT + y
        arrived(e2r.at[dd], e2_recv.at[dd])
        arrived(e3r.at[zz], e3_recv.at[zz])
        value = keep2[dd] + e2r[dd].astype(f32) + e3r[zz].astype(f32)
        if k < Z_COUNT - 1:
            e4s[zz] = value.astype(bf16)
            send(e4s.at[zz], e4r.at[z], e4_send.at[zz], e4_recv.at[z], (dd, t))
        else:
            result = result + value
    for step in range(1, Z_COUNT):
        other = z_at(step)
        arrived(e4r.at[other], e4_recv.at[other])
        result = result + e4r[other].astype(f32)
    halves = []
    for cc in range(CORES):
        near, far = cc * share, cc * share + 64
        shifted = pltpu.roll(result, WINDOW - far, 1)
        base = pltpu.roll(result, WINDOW - near, 1) if near else result
        halves.append(jnp.where(x == 0, base, shifted)[:, 0:256].astype(bf16))
    fsend[...] = jnp.where(c == 0, halves[1].astype(f32), halves[0].astype(f32)).astype(bf16)
    send(fsend, frecv, f_send.at[0], f_recv.at[0], core_peer)
    mine = jnp.where(c == 0, halves[0].astype(f32), halves[1].astype(f32)).astype(bf16)
    out_ref[c] = mine[:, 0:share]
    arrived(frecv, f_recv.at[0])
    out_ref[1 - c] = frecv[:, 0:share]

    for step in range(1, dp_count):
        sent(outg.at[own_rows(lax.rem(d + step, dp_count))], a_send.at[step])
    for chunk in range(CHUNKS):
        for number in range(8):
            if number != 4:
                sent(hbuf.at[chunk, d], b_send.at[chunk, number])
    for step in range(1, 4):
        sent(csend.at[lax.rem(t + step, 4)], c_send.at[step])
    for kind, numbers in ((0, range(1, 4)), (1, range(4)), (2, range(8)), (3, range(16))):
        for number in numbers:
            sent(xbuf.at[own, c], d_send.at[kind, number])
    for dd in range(dp_count):
        sent(e1s.at[dd], e1_send.at[dd])
        sent(e2s.at[dd], e2_send.at[dd])
    for zz in range(Z_COUNT):
        sent(e3s.at[zz], e3_send.at[zz])
    for step in range(1, Z_COUNT):
        sent(e4s.at[z_at(step)], e4_send.at[z_at(step)])
    sent(fsend, f_send.at[0])


def fused_shards(
    prefill_latent,
    request_slot,
    new_lengths,
    ctx_lengths,
    kv_cache,
    queries,
    step_latents,
    w_uv,
    w_out,
    hidden,
    ffn_gain,
    w_gate,
    w_up,
    w_down,
):
    f32, bf16 = jnp.float32, jnp.bfloat16
    width = queries.shape[3]
    heads = queries.shape[2]
    ff_share = w_down.shape[0]
    prefill_latent = prefill_latent.T
    new_lengths = new_lengths.T
    kv_cache = kv_cache.transpose(0, 2, 1)
    w_gate = w_gate.T
    w_up = w_up.T
    gain = ffn_gain.reshape(-1, 128)
    smem = pl.BlockSpec(memory_space=pltpu.SMEM)
    vmem = pl.BlockSpec(memory_space=pltpu.VMEM)
    hbm = pl.BlockSpec(memory_space=pl.ANY)
    dma = pltpu.SemaphoreType.DMA
    pieces = (32, WINDOW)
    scratch = [
        pltpu.VMEM(prefill_latent.shape, bf16),
        pltpu.VMEM(kv_cache.shape, bf16),
        pltpu.VMEM(queries.shape, bf16),
        pltpu.VMEM(step_latents.shape, bf16),
        pltpu.VMEM(w_uv.shape, bf16),
        pltpu.VMEM(w_out.shape, bf16),
        pltpu.VMEM(hidden.shape, bf16),
        pltpu.VMEM(w_gate.shape, bf16),
        pltpu.VMEM(w_up.shape, bf16),
        pltpu.VMEM(w_down.shape, bf16),
        pltpu.VMEM((prefill_latent.shape[1] + 128, width), bf16),
        pltpu.VMEM((prefill_latent.shape[1], width), bf16),
        pltpu.VMEM((4, 2 * heads, kv_cache.shape[2]), f32),
        pltpu.VMEM((LAT // 128, heads * 8, 128), f32),
        pltpu.VMEM((CHUNKS, 8, 16, heads // 2 // CHUNKS * 128), bf16),
        pltpu.VMEM((4, *pieces), f32),
        pltpu.VMEM((4, *pieces), bf16),
        pltpu.VMEM((4, *pieces), bf16),
        pltpu.VMEM((2, 32, w_out.shape[2]), f32),
        pltpu.VMEM(pieces, f32),
        pltpu.VMEM((16, 2, *pieces), bf16),
        pltpu.VMEM((ff_share, 64), f32),
        pltpu.VMEM((ff_share, 64), f32),
        pltpu.VMEM((2, 64, 128), f32),
        pltpu.VMEM((64, ff_share), bf16),
        pltpu.VMEM((8, 2, *pieces), bf16),
        pltpu.VMEM((8, 2, *pieces), bf16),
        pltpu.VMEM((8, 2, *pieces), f32),
        pltpu.VMEM((8, *pieces), bf16),
        pltpu.VMEM((8, *pieces), bf16),
        pltpu.VMEM((8, *pieces), f32),
        pltpu.VMEM((4, *pieces), bf16),
        pltpu.VMEM((4, *pieces), bf16),
        pltpu.VMEM((4, *pieces), bf16),
        pltpu.VMEM((4, *pieces), bf16),
        pltpu.VMEM((32, 256), bf16),
        pltpu.VMEM((32, 256), bf16),
        dma((16,)),
        dma((8,)),
        dma((8,)),
        dma((CHUNKS, 8)),
        dma((CHUNKS, 8)),
        dma((4,)),
        dma((4,)),
        dma((4, 16)),
        dma((32,)),
        dma((8,)),
        dma((8,)),
        dma((8,)),
        dma((8,)),
        dma((4,)),
        dma((4,)),
        dma((4,)),
        dma((4,)),
        dma((1,)),
        dma((1,)),
    ]
    return pl.pallas_call(
        layer_kernel,
        out_shape=jax.ShapeDtypeStruct(hidden.shape, bf16),
        in_specs=[smem] * 3 + [hbm] * 7 + [vmem] + [hbm] * 3,
        out_specs=vmem,
        scratch_shapes=scratch,
        compiler_params=pltpu.CompilerParams(
            collective_id=0, has_side_effects=True, vmem_limit_bytes=60 * 1024 * 1024
        ),
        cost_estimate=pl.CostEstimate(
            flops=4_000_000_000, bytes_accessed=42_000_000, transcendentals=400_000
        ),
    )(
        request_slot,
        new_lengths,
        ctx_lengths,
        prefill_latent,
        kv_cache,
        queries,
        step_latents,
        w_uv,
        w_out,
        hidden,
        gain,
        w_gate,
        w_up,
        w_down,
    )


def shards(dp_count, tp_count, *arrays):
    if (dp_count, tp_count) == (Z_COUNT * Y_COUNT, X_COUNT * CORES):
        return fused_shards(*arrays)
    return plain_shards(*arrays)


def solution(mesh):
    return jax.shard_map(
        functools.partial(shards, mesh.shape["dp"], mesh.shape["tp"]),
        mesh=mesh,
        in_specs=(
            P("dp", None),
            P(),
            P(),
            P("dp"),
            P("dp", None, None),
            P(None, "dp", "tp", None),
            P(None, "dp", None),
            P("tp", None, None),
            P("tp", None, "dp"),
            P(None, None, ("dp", "tp")),
            P(),
            P(None, ("dp", "tp")),
            P(None, ("dp", "tp")),
            P(("dp", "tp"), None),
        ),
        out_specs=P(None, None, ("dp", "tp")),
        check_vma=False,
    )
```

```python
import functools

import jax
import jax.numpy as jnp
from jax import lax
from jax.experimental import pallas as pl
from jax.experimental.pallas import tpu as pltpu
from jax.sharding import PartitionSpec as P

LAT = 512
QKD = 192
OWN_TOK = 16


masked_score = -1e30
norm_eps = 1e-06


def attend(query, step_ids, kv_cache, cache_mask, new_rows, new_mask, step_latents, w_uv):
    score_scale = QKD ** (-0.5)
    cache_scores = (
        jnp.einsum("sqhc,qkc->sqhk", query, kv_cache, preferred_element_type=jnp.float32)
        * score_scale
    )
    cache_scores = jnp.where(cache_mask[None, :, None, :], cache_scores, masked_score)
    fresh_scores = (
        jnp.einsum("sqhc,kc->sqhk", query, new_rows, preferred_element_type=jnp.float32)
        * score_scale
    )
    fresh_scores = jnp.where(new_mask[None, :, None, :], fresh_scores, masked_score)
    token_scores = (
        jnp.einsum("sqhc,tqc->sqht", query, step_latents, preferred_element_type=jnp.float32)
        * score_scale
    )
    token_valid = jnp.arange(step_latents.shape[0], dtype=jnp.int32)[None, :] <= step_ids[:, None]
    token_scores = jnp.where(token_valid[:, None, None, :], token_scores, masked_score)
    highest = jnp.maximum(
        jnp.maximum(jnp.max(cache_scores, axis=-1), jnp.max(fresh_scores, axis=-1)),
        jnp.max(token_scores, axis=-1),
    )[..., None]
    cache_exp = jnp.exp(cache_scores - highest)
    fresh_exp = jnp.exp(fresh_scores - highest)
    token_exp = jnp.exp(token_scores - highest)
    totals = (
        jnp.sum(cache_exp, axis=-1, keepdims=True)
        + jnp.sum(fresh_exp, axis=-1, keepdims=True)
        + jnp.sum(token_exp, axis=-1, keepdims=True)
    )
    cache_probs = (cache_exp / totals).astype(jnp.bfloat16)
    fresh_probs = (fresh_exp / totals).astype(jnp.bfloat16)
    token_probs = (token_exp / totals).astype(jnp.bfloat16)
    latent_out = jnp.einsum(
        "sqhk,qkc->sqhc", cache_probs, kv_cache[:, :, :LAT], preferred_element_type=jnp.float32
    )
    latent_out = latent_out + jnp.einsum(
        "sqhk,kc->sqhc", fresh_probs, new_rows[:, :LAT], preferred_element_type=jnp.float32
    )
    latent_out = latent_out + jnp.einsum(
        "sqht,tqc->sqhc", token_probs, step_latents[:, :, :LAT], preferred_element_type=jnp.float32
    )
    latent_out = latent_out.astype(jnp.bfloat16)
    return jnp.einsum(
        "sqhc,hcv->sqhv", latent_out, w_uv, preferred_element_type=jnp.float32
    ).astype(jnp.bfloat16)


def plain_shards(
    prefill_latent,
    request_slot,
    new_lengths,
    ctx_lengths,
    kv_cache,
    queries,
    step_latents,
    w_uv,
    w_out,
    hidden,
    ffn_gain,
    w_gate,
    w_up,
    w_down,
):
    dp_count = lax.axis_size("dp")
    dp_rank = lax.axis_index("dp")
    tp_rank = lax.axis_index("tp")
    per_owner = new_lengths.shape[1]
    total_requests = request_slot.shape[0]
    latent_width = kv_cache.shape[2]
    share_width = hidden.shape[2]
    block_width = w_out.shape[2]
    model_width = block_width * dp_count
    numbers = jnp.arange(total_requests, dtype=jnp.int32)
    one_hot = request_slot[:, None] == numbers[None, :]
    lengths_flat = new_lengths.reshape(-1)
    request_rows = jnp.sum(jnp.where(one_hot, lengths_flat[None, :], 0), axis=1)
    offsets = jnp.cumsum(request_rows) - request_rows
    inverse = jnp.sum(jnp.where(one_hot, numbers[:, None], 0), axis=0)
    slot_start = jnp.cumsum(new_lengths, axis=1) - new_lengths
    positions = jnp.arange(OWN_TOK, dtype=jnp.int32)
    slot_of_place = (
        jnp.sum((slot_start[:, :, None] <= positions[None, None, :]).astype(jnp.int32), axis=1) - 1
    )
    owner_ids = jnp.arange(dp_count, dtype=jnp.int32)[:, None]
    owner_rows = owner_ids * per_owner + slot_of_place
    start_in_slot = jnp.take_along_axis(slot_start, slot_of_place, axis=1)
    source_rows = (
        jnp.take(offsets, jnp.take(inverse, owner_rows)) + positions[None, :] - start_in_slot
    )
    outgoing = jnp.take(prefill_latent, source_rows.reshape(-1), axis=0).reshape(
        dp_count, OWN_TOK, latent_width
    )
    incoming = lax.all_to_all(outgoing, "dp", split_axis=0, concat_axis=0, tiled=True)
    new_rows = incoming.reshape(dp_count * OWN_TOK, latent_width)
    my_lengths = lax.dynamic_index_in_dim(new_lengths, dp_rank, 0, keepdims=False)
    my_start = jnp.cumsum(my_lengths) - my_lengths
    in_slot = (positions[None, :] >= my_start[:, None]) & (
        positions[None, :] < (my_start + my_lengths)[:, None]
    )
    new_mask = jnp.tile(in_slot, (1, dp_count))
    cache_mask = jnp.arange(kv_cache.shape[1], dtype=jnp.int32)[None, :] < ctx_lengths[:, None]
    share_first = tp_rank * share_width

    def finish(first, last):
        step_ids = jnp.arange(first, last, dtype=jnp.int32)
        steps_here = last - first
        head_out = attend(
            queries[first:last],
            step_ids,
            kv_cache,
            cache_mask,
            new_rows,
            new_mask,
            step_latents,
            w_uv,
        )
        every_row = lax.all_gather(head_out, "dp", axis=1, tiled=True)
        partial_value = jnp.dot(
            every_row.reshape(steps_here * total_requests, -1),
            w_out.reshape(-1, block_width),
            preferred_element_type=jnp.float32,
        )
        partial_value = partial_value.reshape(steps_here, total_requests, block_width)
        own_cols = lax.dynamic_slice_in_dim(partial_value, share_first, share_width, 2) + hidden[
            first:last
        ].astype(jnp.float32)
        partial_value = lax.dynamic_update_slice_in_dim(partial_value, own_cols, share_first, 2)
        mixed = lax.psum_scatter(partial_value, "tp", scatter_dimension=2, tiled=True)
        squares = lax.psum(jnp.sum(mixed * mixed, axis=-1), ("dp", "tp"))
        gain_part = lax.dynamic_slice_in_dim(
            ffn_gain, dp_rank * block_width + share_first, share_width
        )
        scaled_part = (mixed * gain_part).astype(jnp.bfloat16)
        scaled = lax.all_gather(scaled_part, ("dp", "tp"), axis=2, tiled=True)
        flat_input = scaled.reshape(steps_here * total_requests, model_width)
        row_scale = lax.rsqrt(squares / model_width + norm_eps).reshape(-1, 1)
        gate_out = jnp.dot(flat_input, w_gate, preferred_element_type=jnp.float32) * row_scale
        up_out = jnp.dot(flat_input, w_up, preferred_element_type=jnp.float32) * row_scale
        activated = (jax.nn.silu(gate_out) * up_out).astype(jnp.bfloat16)
        down_out = jnp.dot(activated, w_down, preferred_element_type=jnp.float32).reshape(
            steps_here, total_requests, model_width
        )
        ffn_part = lax.psum_scatter(down_out, ("dp", "tp"), scatter_dimension=2, tiled=True)
        return (mixed + ffn_part).astype(jnp.bfloat16)

    return finish(0, queries.shape[0])


Z_COUNT, Y_COUNT, X_COUNT, CORES = 4, 2, 2, 2
CHUNKS = 4
WINDOW = 512


def dot_f32(left, right):
    return jnp.dot(left, right, preferred_element_type=jnp.float32)


def dot_rows(left, right):
    return lax.dot_general(
        left, right, (((1,), (1,)), ((), ())), preferred_element_type=jnp.float32
    )


def layer_kernel(
    slot_s,
    len_s,
    ctx_s,
    pre_h,
    kv_h,
    qry_h,
    stp_h,
    uv_h,
    wo_h,
    hid_h,
    gain_v,
    wg_h,
    wu_h,
    wd_h,
    out_ref,
    pre,
    kv,
    qry,
    stp,
    uv,
    wo,
    hid,
    wg,
    wu,
    wd,
    tail,
    outg,
    score,
    lat,
    hbuf,
    cpart,
    csend,
    crecv,
    hidw,
    mixed_v,
    xbuf,
    gacc,
    uacc,
    sqacc,
    act,
    e1s,
    e1r,
    keep1,
    e2s,
    e2r,
    keep2,
    e3s,
    e3r,
    e4s,
    e4r,
    fsend,
    frecv,
    cache_out,
    load_sem,
    a_send,
    a_recv,
    b_send,
    b_recv,
    c_send,
    c_recv,
    d_send,
    d_recv,
    e1_send,
    e1_recv,
    e2_send,
    e2_recv,
    e3_send,
    e3_recv,
    e4_send,
    e4_recv,
    f_send,
    f_recv,
):
    f32, bf16 = jnp.float32, jnp.bfloat16
    dp_count = Z_COUNT * Y_COUNT
    d = lax.axis_index("dp")
    t = lax.axis_index("tp")
    z, y = lax.div(d, Y_COUNT), lax.rem(d, Y_COUNT)
    x, c = lax.div(t, CORES), lax.rem(t, CORES)
    heads = qry.shape[2]
    share = hid.shape[2]
    block_width = 4 * share
    rows = 2 * 4 * dp_count
    y_peer = (z * Y_COUNT + (1 - y), t)
    x_peer = (d, (1 - x) * CORES + c)
    core_peer = (d, x * CORES + (1 - c))

    def z_at(step):
        return lax.rem(z + step, Z_COUNT)

    def send(src, dst, send_sem, recv_sem, device):
        copy = pltpu.make_async_remote_copy(
            src_ref=src,
            dst_ref=dst,
            send_sem=send_sem,
            recv_sem=recv_sem,
            device_id=device,
            device_id_type=pl.DeviceIdType.MESH,
        )
        copy.start()

    def arrived(ref, sem):
        pltpu.make_async_remote_copy(
            src_ref=ref,
            dst_ref=ref,
            send_sem=sem,
            recv_sem=sem,
            device_id=y_peer,
            device_id_type=pl.DeviceIdType.MESH,
        ).wait_recv()

    def sent(ref, sem):
        pltpu.make_async_remote_copy(
            src_ref=ref,
            dst_ref=ref,
            send_sem=sem,
            recv_sem=sem,
            device_id=y_peer,
            device_id_type=pl.DeviceIdType.MESH,
        ).wait_send()

    barrier = pltpu.get_barrier_semaphore()
    for step in range(1, dp_count):
        pl.semaphore_signal(
            barrier,
            inc=1,
            device_id=(lax.rem(d + step, dp_count), t),
            device_id_type=pl.DeviceIdType.MESH,
        )
    for step in range(1, 4):
        pl.semaphore_signal(
            barrier,
            inc=1,
            device_id=(d, lax.rem(t + step, 4)),
            device_id_type=pl.DeviceIdType.MESH,
        )

    def load(index, src, dst):
        copy = pltpu.make_async_copy(src, dst, load_sem.at[index])
        copy.start()
        return copy

    load_pre = load(0, pre_h, pre)
    load_stp = load(1, stp_h, stp)
    load_qry = load(2, qry_h, qry)
    load_kv = [load(3 + i, kv_h.at[i], kv.at[i]) for i in range(4)]
    load_hid = load(7, hid_h, hid)
    load_uv = load(8, uv_h, uv)

    pf_rows = pre.shape[1]
    source = lax.broadcasted_iota(jnp.int32, (8, pf_rows), 1)

    def place_request(r, carry):
        dest, offset = carry
        owner_row = slot_s[r]
        owner = lax.shift_right_logical(owner_row, 2)
        place = owner_row & 3
        count = len_s[place, owner]
        start = jnp.int32(0)
        for k in range(3):
            start = start + jnp.where(place > k, len_s[k, owner], 0)
        inside = (source >= offset) & (source < offset + count)
        dest = jnp.where(inside, source + (owner * OWN_TOK + start - offset), dest)
        return dest, offset + count

    dest, _ = lax.fori_loop(
        0, 4 * dp_count, place_request, (jnp.full((8, pf_rows), -1, jnp.int32), jnp.int32(0))
    )
    target = lax.broadcasted_iota(jnp.int32, (pf_rows, pf_rows), 0)
    pick = jnp.where(target == dest[0:1], 1.0, 0.0).astype(bf16)
    load_pre.wait()
    outg[...] = dot_rows(pick, pre[...]).astype(bf16)
    pl.semaphore_wait(barrier, dp_count - 1 + 3)

    def own_rows(index):
        return pl.ds(pl.multiple_of(index * OWN_TOK, OWN_TOK), OWN_TOK)

    for step in range(1, dp_count):
        other = lax.rem(d + step, dp_count)
        send(
            outg.at[own_rows(other)],
            tail.at[own_rows(d)],
            a_send.at[step],
            a_recv.at[d],
            (other, t),
        )
    tail[own_rows(d), :] = outg[own_rows(d), :]
    load_stp.wait()
    tokens = jnp.concatenate(
        [
            stp[0].astype(f32),
            stp[1].astype(f32),
            jnp.zeros((tail.shape[0] - pf_rows - 8, stp.shape[2]), f32),
        ],
        axis=0,
    )
    tail[pf_rows:, :] = tokens.astype(bf16)

    load_qry.wait()
    key_block = 256
    for i in range(4):
        load_kv[i].wait()
        query = jnp.concatenate([qry[0, i], qry[1, i]], axis=0)
        for k in range(kv.shape[2] // key_block):
            part = slice(k * key_block, (k + 1) * key_block)
            score[i, :, part] = dot_f32(query, kv[i, :, part])
        if i == 1:
            load_wo = load(9, wo_h, wo)
    load_wg = load(10, wg_h, wg)
    load_wu = load(11, wu_h, wu)
    load_wd = load(12, wd_h, wd)

    load_hid.wait()
    hidw[...] = jnp.zeros_like(hidw)
    for s in range(2):
        hidw[s, :, 0:share] = hid[s].astype(f32)
    for s in range(2):
        narrow = hidw[s]
        placed = narrow
        for k in range(1, 4):
            placed = jnp.where(t == k, pltpu.roll(narrow, k * share, 1), placed)
        hidw[s] = placed

    scale = QKD ** (-0.5)
    q_rows = 2 * heads
    key_col = lax.broadcasted_iota(jnp.int32, (q_rows, kv.shape[2]), 1)
    cache_max, cache_sum = [], []
    for i in range(4):
        cache_score = jnp.where(key_col < ctx_s[i], score[i] * scale, masked_score)
        top = jnp.max(cache_score, axis=1, keepdims=True)
        cache_exp = jnp.exp(cache_score - top)
        cache_max.append(top)
        cache_sum.append(jnp.sum(cache_exp, axis=1, keepdims=True))
        cache_out[i] = jnp.transpose(dot_rows(kv[i, 0:LAT, :], cache_exp.astype(bf16)))

    for step in range(1, dp_count):
        other = lax.rem(d + step, dp_count)
        arrived(tail.at[own_rows(other)], a_recv.at[other])

    tail_col = lax.broadcasted_iota(jnp.int32, (q_rows, tail.shape[0]), 1)
    tail_step = lax.broadcasted_iota(jnp.int32, (q_rows, tail.shape[0]), 0) // heads
    spot = tail_col & (OWN_TOK - 1)
    token = tail_col - pf_rows
    token_place = token & 3
    token_ok = (token >= 0) & (token < 8) & (lax.shift_right_arithmetic(token, 2) <= tail_step)
    start = jnp.int32(0)
    for i in range(4):
        count = len_s[i, d]
        query = jnp.concatenate([qry[0, i], qry[1, i]], axis=0)
        tail_score = dot_rows(query, tail[...]) * scale
        fresh_ok = (tail_col < pf_rows) & (spot >= start) & (spot < start + count)
        start = start + count
        tail_score = jnp.where(
            fresh_ok | (token_ok & (token_place == i)), tail_score, masked_score
        )
        tail_max = jnp.max(tail_score, axis=1, keepdims=True)
        tail_exp = jnp.exp(tail_score - tail_max)
        tail_sum = jnp.sum(tail_exp, axis=1, keepdims=True)
        highest = jnp.maximum(cache_max[i], tail_max)
        cache_part = jnp.exp(cache_max[i] - highest)
        tail_part = jnp.exp(tail_max - highest)
        total = cache_sum[i] * cache_part + tail_sum * tail_part
        latent = cache_out[i] * (cache_part / total) + dot_f32(
            tail_exp.astype(bf16), tail[:, :LAT]
        ) * (tail_part / total)
        for s in range(2):
            for b in range(LAT // 128):
                lat[b, pl.ds(s * 4 + i, heads, stride=8), :] = latent[
                    s * heads : (s + 1) * heads, b * 128 : (b + 1) * 128
                ]

    half = heads // 2
    per_chunk = half // CHUNKS
    load_uv.wait()

    def head_rows(h):
        return jnp.concatenate(
            [lat[b, h * 8 : (h + 1) * 8, :] for b in range(LAT // 128)], axis=1
        )

    def forward_heads(chunk):
        for step in range(1, Z_COUNT):
            other = z_at(step) * Y_COUNT + y
            arrived(hbuf.at[chunk, other], b_recv.at[chunk, other])
            send(
                hbuf.at[chunk, other],
                hbuf.at[chunk, other],
                b_send.at[chunk, 4 + step],
                b_recv.at[chunk, other],
                y_peer,
            )

    for chunk in range(CHUNKS):
        outs = []
        for p in range(per_chunk):
            h = chunk * per_chunk + p
            both = jnp.concatenate([head_rows(h), head_rows(h + half)], axis=0).astype(bf16)
            low_out = dot_f32(both, uv[h])[0:8]
            high_out = dot_f32(both, uv[h + half])[8:16]
            outs.append(jnp.concatenate([low_out, high_out], axis=0).astype(bf16))
        hbuf[chunk, d] = jnp.concatenate(outs, axis=1)
        for step in range(1, Z_COUNT):
            send(
                hbuf.at[chunk, d],
                hbuf.at[chunk, d],
                b_send.at[chunk, step],
                b_recv.at[chunk, d],
                (z_at(step) * Y_COUNT + y, t),
            )
        send(
            hbuf.at[chunk, d],
            hbuf.at[chunk, d],
            b_send.at[chunk, 0],
            b_recv.at[chunk, d],
            y_peer,
        )
        if chunk >= 1:
            forward_heads(chunk - 1)
    forward_heads(CHUNKS - 1)

    load_wo.wait()
    out_sum = None
    for chunk in range(CHUNKS):
        for step in range(Z_COUNT):
            other = z_at(step) * Y_COUNT + (1 - y)
            arrived(hbuf.at[chunk, other], b_recv.at[chunk, other])
        left = hbuf[chunk].reshape(dp_count * 16, per_chunk * 128)
        for a in range(2):
            first = a * half + chunk * per_chunk
            weight = wo[first : first + per_chunk].reshape(per_chunk * 128, block_width)
            product = dot_f32(left, weight).reshape(dp_count, 16, block_width)
            product = product[:, a * 8 : (a + 1) * 8, :]
            out_sum = product if out_sum is None else out_sum + product
    partial = []
    for s in range(2):
        tiles = []
        for k in range(dp_count):
            tiles.append(out_sum[k, s * 4 : s * 4 + 4])
        partial.append(jnp.concatenate(tiles, axis=0) + hidw[s])
    for xx in range(X_COUNT):
        for cc in range(CORES):
            piece = partial[cc][:, xx * 384 : xx * 384 + WINDOW]
            cpart[xx * CORES + cc] = piece
            csend[xx * CORES + cc] = piece.astype(bf16)
    for step in range(1, 4):
        other = lax.rem(t + step, 4)
        send(csend.at[other], crecv.at[t], c_send.at[step], c_recv.at[t], (d, other))
    gain = jnp.concatenate(
        [gain_v[pl.ds(d * (block_width // 128) + x * 3 + k, 1), :] for k in range(4)], axis=1
    )
    mixed = cpart[t]
    for step in range(1, 4):
        other = lax.rem(t + step, 4)
        arrived(crecv.at[other], c_recv.at[other])
        mixed = mixed + crecv[other].astype(f32)
    lanes = lax.broadcasted_iota(jnp.int32, mixed.shape, 1)
    pair = 2 * share
    mixed = jnp.where((lanes >= 64 * x) & (lanes < 64 * x + pair), mixed, 0.0)
    mixed_v[...] = mixed
    squares = jnp.sum(mixed * mixed, axis=1, keepdims=True)
    squares_high = squares.astype(bf16).astype(f32)
    spare = pair * (1 - x)
    own_block = mixed * gain
    own_block = jnp.where(lanes == spare, squares_high, own_block)
    own_block = jnp.where(lanes == spare + 1, squares - squares_high, own_block)

    def slot_of(xx, yy, zz):
        return (xx * Y_COUNT + yy) * Z_COUNT + zz

    own = slot_of(x, y, z)
    xbuf[own, c] = own_block.astype(bf16)

    def pass_on(slot, kind, number, device):
        send(
            xbuf.at[slot, c],
            xbuf.at[slot, c],
            d_send.at[kind, number],
            d_recv.at[slot * 2 + c],
            device,
        )

    for step in range(1, Z_COUNT):
        pass_on(own, 0, step, (z_at(step) * Y_COUNT + y, t))
    pass_on(own, 1, 0, y_peer)
    pass_on(own, 2, 0, x_peer)
    pass_on(own, 3, 0, core_peer)

    gacc[...] = jnp.zeros_like(gacc)
    uacc[...] = jnp.zeros_like(uacc)
    sqacc[...] = jnp.zeros_like(sqacc)
    load_wg.wait()
    load_wu.wait()
    block_lane = lax.broadcasted_iota(jnp.int32, (rows, WINDOW), 1)

    def use_block(xx, yy, zz):
        slot = slot_of(xx, yy, zz)
        arrived(xbuf.at[slot, 1 - c], d_recv.at[slot * 2 + (1 - c)])
        block = xbuf[slot].reshape(rows, WINDOW).astype(f32)
        inside = (block_lane >= 64 * xx) & (block_lane < 64 * xx + pair)
        block = jnp.where(inside, block, 0.0).astype(bf16)
        first = pl.multiple_of((zz * Y_COUNT + yy) * block_width + xx * 384, 128)
        gacc[...] += dot_rows(wg[:, pl.ds(first, WINDOW)], block)
        uacc[...] += dot_rows(wu[:, pl.ds(first, WINDOW)], block)
        lane = pl.multiple_of(384 * (1 - xx), 128)
        sqacc[xx] += xbuf[slot, :, :, pl.ds(lane, 128)].reshape(rows, 128).astype(f32)

    def take(xx, yy, zz):
        slot = slot_of(xx, yy, zz)
        arrived(xbuf.at[slot, c], d_recv.at[slot * 2 + c])
        return slot

    def from_z(m, carry):
        slot = take(x, y, z_at(m))
        pass_on(slot, 1, m, y_peer)
        pass_on(slot, 2, m, x_peer)
        pass_on(slot, 3, m, core_peer)
        return carry

    def from_sides(m):
        zz = z_at(m)
        odd = lax.rem(zz, 2)
        by_y = take(x, 1 - y, zz)

        @pl.when(odd == 0)
        def _():
            pass_on(by_y, 2, 4 + lax.div(zz, 2), x_peer)

        pass_on(by_y, 3, 4 + m, core_peer)
        by_x = take(1 - x, y, zz)

        @pl.when(odd == 1)
        def _():
            pass_on(by_x, 1, 4 + lax.div(zz, 2), y_peer)

        pass_on(by_x, 3, 8 + m, core_peer)

    def from_sides_and_use(m, carry):
        from_sides(m)
        use_block(x, y, z_at(m))
        return carry

    def from_corner_and_use(m, carry):
        zz = z_at(m)
        pass_on(take(1 - x, 1 - y, zz), 3, 12 + m, core_peer)
        use_block(x, 1 - y, zz)
        use_block(1 - x, y, zz)
        return carry

    def use_corner(m, carry):
        use_block(1 - x, 1 - y, z_at(m))
        return carry

    use_block(x, y, z)
    lax.fori_loop(1, Z_COUNT, from_z, 0)
    from_sides(jnp.int32(0))
    lax.fori_loop(1, Z_COUNT, from_sides_and_use, 0)
    lax.fori_loop(0, Z_COUNT, from_corner_and_use, 0)
    lax.fori_loop(0, Z_COUNT, use_corner, 0)

    sq_lane = lax.broadcasted_iota(jnp.int32, (rows, 128), 1)
    sq_all = jnp.where((sq_lane == pair - 384) | (sq_lane == pair - 383), sqacc[0], 0.0)
    sq_all = sq_all + jnp.where(sq_lane < 2, sqacc[1], 0.0)
    sq_total = jnp.sum(jnp.transpose(sq_all), axis=0, keepdims=True)
    token_scale = lax.rsqrt(sq_total / (block_width * dp_count) + norm_eps)
    gate = gacc[...] * token_scale
    hidden_units = gate / (1.0 + jnp.exp(-gate)) * (uacc[...] * token_scale)
    by_token = jnp.transpose(hidden_units)
    act[0:32] = jnp.where(c == 0, by_token[0:32], by_token[32:64]).astype(bf16)
    act[32:64] = jnp.where(c == 0, by_token[32:64], by_token[0:32]).astype(bf16)

    load_wd.wait()

    def dest_dp(i):
        yy = lax.rem(y + 1 + lax.div(i, Z_COUNT), 2)
        return z_at(1 + lax.rem(i, Z_COUNT)) * Y_COUNT + yy

    def first_turn(i):
        dd = dest_dp(i)
        zz = lax.div(dd, Y_COUNT)
        odd = lax.rem(zz, 2)
        arrived(e1r.at[dd], e1_recv.at[dd])

        def summed(xx):
            return keep1[dd, xx] + e1r[dd, xx].astype(f32)

        @pl.when(odd == 0)
        def _():
            e2s[dd] = summed(1 - x).astype(bf16)
            send(e2s.at[dd], e2r.at[dd], e2_send.at[dd], e2_recv.at[dd], x_peer)
            keep2[dd] = summed(x)

        @pl.when((odd == 1) & (i < Z_COUNT))
        def _():
            for xx in range(X_COUNT):
                k = zz * 2 + xx
                e2s[k] = summed(xx).astype(bf16)
                send(e2s.at[k], e2r.at[k], e2_send.at[k], e2_recv.at[k], y_peer)

        @pl.when((odd == 1) & (i >= Z_COUNT))
        def _():
            for xx in range(X_COUNT):
                keep2[zz * 2 + xx] = summed(xx)

    def down(i, carry):
        dd = dest_dp(i)
        first = pl.multiple_of(dd * block_width, 128)
        product = dot_f32(act[...], wd[:, pl.ds(first, block_width)])
        for xx in range(X_COUNT):
            window = slice(xx * 384, xx * 384 + WINDOW)
            keep1[dd, xx] = product[0:32, window]
            e1s[dd, xx] = product[32:64, window].astype(bf16)
        send(e1s.at[dd], e1r.at[dd], e1_send.at[dd], e1_recv.at[dd], core_peer)

        @pl.when(i >= 2)
        def _():
            first_turn(i - 2)

        return carry

    lax.fori_loop(0, dp_count, down, 0)
    first_turn(jnp.int32(dp_count - 2))
    first_turn(jnp.int32(dp_count - 1))
    for k in range(Z_COUNT):
        zz = z_at(1 + k)
        odd = lax.rem(zz, 2)
        sent_part = zz * 2 + (1 - y) + odd * (y - x)
        arrived(e2r.at[sent_part], e2_recv.at[sent_part])
        e3s[zz] = (keep2[sent_part] + e2r[sent_part].astype(f32)).astype(bf16)
        peer_y = y + (1 - odd) * (1 - 2 * y)
        peer_x = x + odd * (1 - 2 * x)
        send(
            e3s.at[zz],
            e3r.at[zz],
            e3_send.at[zz],
            e3_recv.at[zz],
            (z * Y_COUNT + peer_y, peer_x * CORES + c),
        )
    result = mixed_v[...]
    for k in range(Z_COUNT):
        zz = z_at(1 + k)
        dd = zz * Y_COUNT + y
        kept_part = zz * 2 + y + lax.rem(zz, 2) * (x - y)
        arrived(e2r.at[kept_part], e2_recv.at[kept_part])
        arrived(e3r.at[zz], e3_recv.at[zz])
        value = keep2[kept_part] + e2r[kept_part].astype(f32) + e3r[zz].astype(f32)
        if k < Z_COUNT - 1:
            e4s[zz] = value.astype(bf16)
            send(e4s.at[zz], e4r.at[z], e4_send.at[zz], e4_recv.at[z], (dd, t))
        else:
            result = result + value
    for step in range(1, Z_COUNT):
        other = z_at(step)
        arrived(e4r.at[other], e4_recv.at[other])
        result = result + e4r[other].astype(f32)
    halves = []
    for cc in range(CORES):
        near, far = cc * share, cc * share + 64
        shifted = pltpu.roll(result, WINDOW - far, 1)
        base = pltpu.roll(result, WINDOW - near, 1) if near else result
        halves.append(jnp.where(x == 0, base, shifted)[:, 0:256].astype(bf16))
    fsend[...] = jnp.where(c == 0, halves[1].astype(f32), halves[0].astype(f32)).astype(bf16)
    send(fsend, frecv, f_send.at[0], f_recv.at[0], core_peer)
    mine = jnp.where(c == 0, halves[0].astype(f32), halves[1].astype(f32)).astype(bf16)
    out_ref[c] = mine[:, 0:share]
    arrived(frecv, f_recv.at[0])
    out_ref[1 - c] = frecv[:, 0:share]

    for step in range(1, dp_count):
        sent(outg.at[own_rows(lax.rem(d + step, dp_count))], a_send.at[step])
    for chunk in range(CHUNKS):
        for number in range(8):
            if number != 4:
                sent(hbuf.at[chunk, d], b_send.at[chunk, number])
    for step in range(1, 4):
        sent(csend.at[lax.rem(t + step, 4)], c_send.at[step])
    for kind, numbers in ((0, range(1, 4)), (1, range(6)), (2, range(6)), (3, range(16))):
        for number in numbers:
            sent(xbuf.at[own, c], d_send.at[kind, number])
    for dd in range(dp_count):
        sent(e1s.at[dd], e1_send.at[dd])
        sent(e2s.at[dd], e2_send.at[dd])
    for zz in range(Z_COUNT):
        sent(e3s.at[zz], e3_send.at[zz])
    for step in range(1, Z_COUNT):
        sent(e4s.at[z_at(step)], e4_send.at[z_at(step)])
    sent(fsend, f_send.at[0])


def fused_shards(
    prefill_latent,
    request_slot,
    new_lengths,
    ctx_lengths,
    kv_cache,
    queries,
    step_latents,
    w_uv,
    w_out,
    hidden,
    ffn_gain,
    w_gate,
    w_up,
    w_down,
):
    f32, bf16 = jnp.float32, jnp.bfloat16
    width = queries.shape[3]
    heads = queries.shape[2]
    ff_share = w_down.shape[0]
    prefill_latent = prefill_latent.T
    new_lengths = new_lengths.T
    kv_cache = kv_cache.transpose(0, 2, 1)
    w_gate = w_gate.T
    w_up = w_up.T
    gain = ffn_gain.reshape(-1, 128)
    smem = pl.BlockSpec(memory_space=pltpu.SMEM)
    vmem = pl.BlockSpec(memory_space=pltpu.VMEM)
    hbm = pl.BlockSpec(memory_space=pl.ANY)
    dma = pltpu.SemaphoreType.DMA
    pieces = (32, WINDOW)
    scratch = [
        pltpu.VMEM(prefill_latent.shape, bf16),
        pltpu.VMEM(kv_cache.shape, bf16),
        pltpu.VMEM(queries.shape, bf16),
        pltpu.VMEM(step_latents.shape, bf16),
        pltpu.VMEM(w_uv.shape, bf16),
        pltpu.VMEM(w_out.shape, bf16),
        pltpu.VMEM(hidden.shape, bf16),
        pltpu.VMEM(w_gate.shape, bf16),
        pltpu.VMEM(w_up.shape, bf16),
        pltpu.VMEM(w_down.shape, bf16),
        pltpu.VMEM((prefill_latent.shape[1] + 128, width), bf16),
        pltpu.VMEM((prefill_latent.shape[1], width), bf16),
        pltpu.VMEM((4, 2 * heads, kv_cache.shape[2]), f32),
        pltpu.VMEM((LAT // 128, heads * 8, 128), f32),
        pltpu.VMEM((CHUNKS, 8, 16, heads // 2 // CHUNKS * 128), bf16),
        pltpu.VMEM((4, *pieces), f32),
        pltpu.VMEM((4, *pieces), bf16),
        pltpu.VMEM((4, *pieces), bf16),
        pltpu.VMEM((2, 32, w_out.shape[2]), f32),
        pltpu.VMEM(pieces, f32),
        pltpu.VMEM((16, 2, *pieces), bf16),
        pltpu.VMEM((ff_share, 64), f32),
        pltpu.VMEM((ff_share, 64), f32),
        pltpu.VMEM((2, 64, 128), f32),
        pltpu.VMEM((64, ff_share), bf16),
        pltpu.VMEM((8, 2, *pieces), bf16),
        pltpu.VMEM((8, 2, *pieces), bf16),
        pltpu.VMEM((8, 2, *pieces), f32),
        pltpu.VMEM((8, *pieces), bf16),
        pltpu.VMEM((8, *pieces), bf16),
        pltpu.VMEM((8, *pieces), f32),
        pltpu.VMEM((4, *pieces), bf16),
        pltpu.VMEM((4, *pieces), bf16),
        pltpu.VMEM((4, *pieces), bf16),
        pltpu.VMEM((4, *pieces), bf16),
        pltpu.VMEM((32, 256), bf16),
        pltpu.VMEM((32, 256), bf16),
        pltpu.VMEM((4, 2 * heads, LAT), f32),
        dma((16,)),
        dma((8,)),
        dma((8,)),
        dma((CHUNKS, 8)),
        dma((CHUNKS, 8)),
        dma((4,)),
        dma((4,)),
        dma((4, 16)),
        dma((32,)),
        dma((8,)),
        dma((8,)),
        dma((8,)),
        dma((8,)),
        dma((4,)),
        dma((4,)),
        dma((4,)),
        dma((4,)),
        dma((1,)),
        dma((1,)),
    ]
    return pl.pallas_call(
        layer_kernel,
        out_shape=jax.ShapeDtypeStruct(hidden.shape, bf16),
        in_specs=[smem] * 3 + [hbm] * 7 + [vmem] + [hbm] * 3,
        out_specs=vmem,
        scratch_shapes=scratch,
        compiler_params=pltpu.CompilerParams(
            collective_id=0, has_side_effects=True, vmem_limit_bytes=60 * 1024 * 1024
        ),
        cost_estimate=pl.CostEstimate(
            flops=4_000_000_000, bytes_accessed=42_000_000, transcendentals=400_000
        ),
    )(
        request_slot,
        new_lengths,
        ctx_lengths,
        prefill_latent,
        kv_cache,
        queries,
        step_latents,
        w_uv,
        w_out,
        hidden,
        gain,
        w_gate,
        w_up,
        w_down,
    )


def shards(dp_count, tp_count, *arrays):
    if (dp_count, tp_count) == (Z_COUNT * Y_COUNT, X_COUNT * CORES):
        return fused_shards(*arrays)
    return plain_shards(*arrays)


def solution(mesh):
    return jax.shard_map(
        functools.partial(shards, mesh.shape["dp"], mesh.shape["tp"]),
        mesh=mesh,
        in_specs=(
            P("dp", None),
            P(),
            P(),
            P("dp"),
            P("dp", None, None),
            P(None, "dp", "tp", None),
            P(None, "dp", None),
            P("tp", None, None),
            P("tp", None, "dp"),
            P(None, None, ("dp", "tp")),
            P(),
            P(None, ("dp", "tp")),
            P(None, ("dp", "tp")),
            P(("dp", "tp"), None),
        ),
        out_specs=P(None, None, ("dp", "tp")),
        check_vma=False,
    )
```

```python
import functools

import jax
import jax.numpy as jnp
from jax import lax
from jax.experimental import pallas as pl
from jax.experimental.pallas import tpu as pltpu
from jax.sharding import PartitionSpec as P

LAT = 512
QKD = 192
OWN_TOK = 16


masked_score = -1e30
norm_eps = 1e-06


def attend(query, step_ids, kv_cache, cache_mask, new_rows, new_mask, step_latents, w_uv):
    score_scale = QKD ** (-0.5)
    cache_scores = (
        jnp.einsum("sqhc,qkc->sqhk", query, kv_cache, preferred_element_type=jnp.float32)
        * score_scale
    )
    cache_scores = jnp.where(cache_mask[None, :, None, :], cache_scores, masked_score)
    fresh_scores = (
        jnp.einsum("sqhc,kc->sqhk", query, new_rows, preferred_element_type=jnp.float32)
        * score_scale
    )
    fresh_scores = jnp.where(new_mask[None, :, None, :], fresh_scores, masked_score)
    token_scores = (
        jnp.einsum("sqhc,tqc->sqht", query, step_latents, preferred_element_type=jnp.float32)
        * score_scale
    )
    token_valid = jnp.arange(step_latents.shape[0], dtype=jnp.int32)[None, :] <= step_ids[:, None]
    token_scores = jnp.where(token_valid[:, None, None, :], token_scores, masked_score)
    highest = jnp.maximum(
        jnp.maximum(jnp.max(cache_scores, axis=-1), jnp.max(fresh_scores, axis=-1)),
        jnp.max(token_scores, axis=-1),
    )[..., None]
    cache_exp = jnp.exp(cache_scores - highest)
    fresh_exp = jnp.exp(fresh_scores - highest)
    token_exp = jnp.exp(token_scores - highest)
    totals = (
        jnp.sum(cache_exp, axis=-1, keepdims=True)
        + jnp.sum(fresh_exp, axis=-1, keepdims=True)
        + jnp.sum(token_exp, axis=-1, keepdims=True)
    )
    cache_probs = (cache_exp / totals).astype(jnp.bfloat16)
    fresh_probs = (fresh_exp / totals).astype(jnp.bfloat16)
    token_probs = (token_exp / totals).astype(jnp.bfloat16)
    latent_out = jnp.einsum(
        "sqhk,qkc->sqhc", cache_probs, kv_cache[:, :, :LAT], preferred_element_type=jnp.float32
    )
    latent_out = latent_out + jnp.einsum(
        "sqhk,kc->sqhc", fresh_probs, new_rows[:, :LAT], preferred_element_type=jnp.float32
    )
    latent_out = latent_out + jnp.einsum(
        "sqht,tqc->sqhc", token_probs, step_latents[:, :, :LAT], preferred_element_type=jnp.float32
    )
    latent_out = latent_out.astype(jnp.bfloat16)
    return jnp.einsum(
        "sqhc,hcv->sqhv", latent_out, w_uv, preferred_element_type=jnp.float32
    ).astype(jnp.bfloat16)


def plain_shards(
    prefill_latent,
    request_slot,
    new_lengths,
    ctx_lengths,
    kv_cache,
    queries,
    step_latents,
    w_uv,
    w_out,
    hidden,
    ffn_gain,
    w_gate,
    w_up,
    w_down,
):
    dp_count = lax.axis_size("dp")
    dp_rank = lax.axis_index("dp")
    tp_rank = lax.axis_index("tp")
    per_owner = new_lengths.shape[1]
    total_requests = request_slot.shape[0]
    latent_width = kv_cache.shape[2]
    share_width = hidden.shape[2]
    block_width = w_out.shape[2]
    model_width = block_width * dp_count
    numbers = jnp.arange(total_requests, dtype=jnp.int32)
    one_hot = request_slot[:, None] == numbers[None, :]
    lengths_flat = new_lengths.reshape(-1)
    request_rows = jnp.sum(jnp.where(one_hot, lengths_flat[None, :], 0), axis=1)
    offsets = jnp.cumsum(request_rows) - request_rows
    inverse = jnp.sum(jnp.where(one_hot, numbers[:, None], 0), axis=0)
    slot_start = jnp.cumsum(new_lengths, axis=1) - new_lengths
    positions = jnp.arange(OWN_TOK, dtype=jnp.int32)
    slot_of_place = (
        jnp.sum((slot_start[:, :, None] <= positions[None, None, :]).astype(jnp.int32), axis=1) - 1
    )
    owner_ids = jnp.arange(dp_count, dtype=jnp.int32)[:, None]
    owner_rows = owner_ids * per_owner + slot_of_place
    start_in_slot = jnp.take_along_axis(slot_start, slot_of_place, axis=1)
    source_rows = (
        jnp.take(offsets, jnp.take(inverse, owner_rows)) + positions[None, :] - start_in_slot
    )
    outgoing = jnp.take(prefill_latent, source_rows.reshape(-1), axis=0).reshape(
        dp_count, OWN_TOK, latent_width
    )
    incoming = lax.all_to_all(outgoing, "dp", split_axis=0, concat_axis=0, tiled=True)
    new_rows = incoming.reshape(dp_count * OWN_TOK, latent_width)
    my_lengths = lax.dynamic_index_in_dim(new_lengths, dp_rank, 0, keepdims=False)
    my_start = jnp.cumsum(my_lengths) - my_lengths
    in_slot = (positions[None, :] >= my_start[:, None]) & (
        positions[None, :] < (my_start + my_lengths)[:, None]
    )
    new_mask = jnp.tile(in_slot, (1, dp_count))
    cache_mask = jnp.arange(kv_cache.shape[1], dtype=jnp.int32)[None, :] < ctx_lengths[:, None]
    share_first = tp_rank * share_width

    def finish(first, last):
        step_ids = jnp.arange(first, last, dtype=jnp.int32)
        steps_here = last - first
        head_out = attend(
            queries[first:last],
            step_ids,
            kv_cache,
            cache_mask,
            new_rows,
            new_mask,
            step_latents,
            w_uv,
        )
        every_row = lax.all_gather(head_out, "dp", axis=1, tiled=True)
        partial_value = jnp.dot(
            every_row.reshape(steps_here * total_requests, -1),
            w_out.reshape(-1, block_width),
            preferred_element_type=jnp.float32,
        )
        partial_value = partial_value.reshape(steps_here, total_requests, block_width)
        own_cols = lax.dynamic_slice_in_dim(partial_value, share_first, share_width, 2) + hidden[
            first:last
        ].astype(jnp.float32)
        partial_value = lax.dynamic_update_slice_in_dim(partial_value, own_cols, share_first, 2)
        mixed = lax.psum_scatter(partial_value, "tp", scatter_dimension=2, tiled=True)
        squares = lax.psum(jnp.sum(mixed * mixed, axis=-1), ("dp", "tp"))
        gain_part = lax.dynamic_slice_in_dim(
            ffn_gain, dp_rank * block_width + share_first, share_width
        )
        scaled_part = (mixed * gain_part).astype(jnp.bfloat16)
        scaled = lax.all_gather(scaled_part, ("dp", "tp"), axis=2, tiled=True)
        flat_input = scaled.reshape(steps_here * total_requests, model_width)
        row_scale = lax.rsqrt(squares / model_width + norm_eps).reshape(-1, 1)
        gate_out = jnp.dot(flat_input, w_gate, preferred_element_type=jnp.float32) * row_scale
        up_out = jnp.dot(flat_input, w_up, preferred_element_type=jnp.float32) * row_scale
        activated = (jax.nn.silu(gate_out) * up_out).astype(jnp.bfloat16)
        down_out = jnp.dot(activated, w_down, preferred_element_type=jnp.float32).reshape(
            steps_here, total_requests, model_width
        )
        ffn_part = lax.psum_scatter(down_out, ("dp", "tp"), scatter_dimension=2, tiled=True)
        return (mixed + ffn_part).astype(jnp.bfloat16)

    return finish(0, queries.shape[0])


Z_COUNT, Y_COUNT, X_COUNT, CORES = 4, 2, 2, 2
CHUNKS = 4
WINDOW = 512


def dot_f32(left, right):
    return jnp.dot(left, right, preferred_element_type=jnp.float32)


def dot_rows(left, right):
    return lax.dot_general(
        left, right, (((1,), (1,)), ((), ())), preferred_element_type=jnp.float32
    )


def layer_kernel(
    slot_s,
    len_s,
    ctx_s,
    pre_h,
    kv_h,
    qry_h,
    stp_h,
    uv_h,
    wo_h,
    hid_h,
    gain_v,
    wg_h,
    wu_h,
    wd_h,
    out_ref,
    pre,
    kv,
    qry,
    stp,
    uv,
    wo,
    hid,
    wg,
    wu,
    wd,
    tail,
    outg,
    score,
    lat,
    hbuf,
    cpart,
    csend,
    crecv,
    hidw,
    mixed_v,
    xbuf,
    gacc,
    uacc,
    sqacc,
    act,
    e1s,
    e1r,
    keep1,
    e2s,
    e2r,
    keep2,
    e3s,
    e3r,
    e4s,
    e4r,
    fsend,
    frecv,
    cache_out,
    load_sem,
    a_send,
    a_recv,
    b_send,
    b_recv,
    c_send,
    c_recv,
    d_send,
    d_recv,
    e1_send,
    e1_recv,
    e2_send,
    e2_recv,
    e3_send,
    e3_recv,
    e4_send,
    e4_recv,
    f_send,
    f_recv,
):
    f32, bf16 = jnp.float32, jnp.bfloat16
    dp_count = Z_COUNT * Y_COUNT
    d = lax.axis_index("dp")
    t = lax.axis_index("tp")
    z, y = lax.div(d, Y_COUNT), lax.rem(d, Y_COUNT)
    x, c = lax.div(t, CORES), lax.rem(t, CORES)
    heads = qry.shape[2]
    share = hid.shape[2]
    block_width = 4 * share
    rows = 2 * 4 * dp_count
    y_peer = (z * Y_COUNT + (1 - y), t)
    x_peer = (d, (1 - x) * CORES + c)
    core_peer = (d, x * CORES + (1 - c))

    def z_at(step):
        return lax.rem(z + step, Z_COUNT)

    def send(src, dst, send_sem, recv_sem, device):
        copy = pltpu.make_async_remote_copy(
            src_ref=src,
            dst_ref=dst,
            send_sem=send_sem,
            recv_sem=recv_sem,
            device_id=device,
            device_id_type=pl.DeviceIdType.MESH,
        )
        copy.start()

    def arrived(ref, sem):
        pltpu.make_async_remote_copy(
            src_ref=ref,
            dst_ref=ref,
            send_sem=sem,
            recv_sem=sem,
            device_id=y_peer,
            device_id_type=pl.DeviceIdType.MESH,
        ).wait_recv()

    def sent(ref, sem):
        pltpu.make_async_remote_copy(
            src_ref=ref,
            dst_ref=ref,
            send_sem=sem,
            recv_sem=sem,
            device_id=y_peer,
            device_id_type=pl.DeviceIdType.MESH,
        ).wait_send()

    barrier = pltpu.get_barrier_semaphore()
    for step in range(1, dp_count):
        pl.semaphore_signal(
            barrier,
            inc=1,
            device_id=(lax.rem(d + step, dp_count), t),
            device_id_type=pl.DeviceIdType.MESH,
        )
    for step in range(1, 4):
        pl.semaphore_signal(
            barrier,
            inc=1,
            device_id=(d, lax.rem(t + step, 4)),
            device_id_type=pl.DeviceIdType.MESH,
        )

    def load(index, src, dst):
        copy = pltpu.make_async_copy(src, dst, load_sem.at[index])
        copy.start()
        return copy

    load_pre = load(0, pre_h, pre)
    load_stp = load(1, stp_h, stp)
    load_qry = load(2, qry_h, qry)
    load_kv = [load(3 + i, kv_h.at[i], kv.at[i]) for i in range(4)]
    load_hid = load(7, hid_h, hid)
    load_uv = load(8, uv_h, uv)

    pf_rows = pre.shape[1]
    source = lax.broadcasted_iota(jnp.int32, (8, pf_rows), 1)

    def place_request(r, carry):
        dest, offset = carry
        owner_row = slot_s[r]
        owner = lax.shift_right_logical(owner_row, 2)
        place = owner_row & 3
        count = len_s[place, owner]
        start = jnp.int32(0)
        for k in range(3):
            start = start + jnp.where(place > k, len_s[k, owner], 0)
        inside = (source >= offset) & (source < offset + count)
        dest = jnp.where(inside, source + (owner * OWN_TOK + start - offset), dest)
        return dest, offset + count

    dest, _ = lax.fori_loop(
        0, 4 * dp_count, place_request, (jnp.full((8, pf_rows), -1, jnp.int32), jnp.int32(0))
    )
    target = lax.broadcasted_iota(jnp.int32, (pf_rows, pf_rows), 0)
    pick = jnp.where(target == dest[0:1], 1.0, 0.0).astype(bf16)
    load_pre.wait()
    outg[...] = dot_rows(pick, pre[...]).astype(bf16)
    pl.semaphore_wait(barrier, dp_count - 1 + 3)

    def own_rows(index):
        return pl.ds(pl.multiple_of(index * OWN_TOK, OWN_TOK), OWN_TOK)

    for step in range(1, dp_count):
        other = lax.rem(d + step, dp_count)
        send(
            outg.at[own_rows(other)],
            tail.at[own_rows(d)],
            a_send.at[step],
            a_recv.at[d],
            (other, t),
        )
    tail[own_rows(d), :] = outg[own_rows(d), :]
    load_stp.wait()
    tokens = jnp.concatenate(
        [
            stp[0].astype(f32),
            stp[1].astype(f32),
            jnp.zeros((tail.shape[0] - pf_rows - 8, stp.shape[2]), f32),
        ],
        axis=0,
    )
    tail[pf_rows:, :] = tokens.astype(bf16)

    load_qry.wait()
    key_block = 256
    for i in range(4):
        load_kv[i].wait()
        query = jnp.concatenate([qry[0, i], qry[1, i]], axis=0)
        for k in range(kv.shape[2] // key_block):
            part = slice(k * key_block, (k + 1) * key_block)
            score[i, :, part] = dot_f32(query, kv[i, :, part])
        if i == 1:
            load_wo = load(9, wo_h, wo)
    load_wg = load(10, wg_h, wg)
    load_wu = load(11, wu_h, wu)
    load_wd = load(12, wd_h, wd)

    load_hid.wait()
    hidw[...] = jnp.zeros_like(hidw)
    for s in range(2):
        hidw[s, :, 0:share] = hid[s].astype(f32)
    for s in range(2):
        narrow = hidw[s]
        placed = narrow
        for k in range(1, 4):
            placed = jnp.where(t == k, pltpu.roll(narrow, k * share, 1), placed)
        hidw[s] = placed

    scale = QKD ** (-0.5)
    q_rows = 2 * heads
    key_col = lax.broadcasted_iota(jnp.int32, (q_rows, kv.shape[2]), 1)
    cache_max, cache_sum = [], []
    for i in range(4):
        cache_score = jnp.where(key_col < ctx_s[i], score[i] * scale, masked_score)
        top = jnp.max(cache_score, axis=1, keepdims=True)
        cache_exp = jnp.exp(cache_score - top)
        cache_max.append(top)
        cache_sum.append(jnp.sum(cache_exp, axis=1, keepdims=True))
        cache_out[i] = dot_rows(cache_exp.astype(bf16), kv[i, 0:LAT, :])

    for step in range(1, dp_count):
        other = lax.rem(d + step, dp_count)
        arrived(tail.at[own_rows(other)], a_recv.at[other])

    tail_col = lax.broadcasted_iota(jnp.int32, (q_rows, tail.shape[0]), 1)
    tail_step = lax.broadcasted_iota(jnp.int32, (q_rows, tail.shape[0]), 0) // heads
    spot = tail_col & (OWN_TOK - 1)
    token = tail_col - pf_rows
    token_place = token & 3
    token_ok = (token >= 0) & (token < 8) & (lax.shift_right_arithmetic(token, 2) <= tail_step)
    start = jnp.int32(0)
    for i in range(4):
        count = len_s[i, d]
        query = jnp.concatenate([qry[0, i], qry[1, i]], axis=0)
        tail_score = dot_rows(query, tail[...]) * scale
        fresh_ok = (tail_col < pf_rows) & (spot >= start) & (spot < start + count)
        start = start + count
        tail_score = jnp.where(
            fresh_ok | (token_ok & (token_place == i)), tail_score, masked_score
        )
        tail_max = jnp.max(tail_score, axis=1, keepdims=True)
        tail_exp = jnp.exp(tail_score - tail_max)
        tail_sum = jnp.sum(tail_exp, axis=1, keepdims=True)
        highest = jnp.maximum(cache_max[i], tail_max)
        cache_part = jnp.exp(cache_max[i] - highest)
        tail_part = jnp.exp(tail_max - highest)
        total = cache_sum[i] * cache_part + tail_sum * tail_part
        latent = cache_out[i] * (cache_part / total) + dot_f32(
            tail_exp.astype(bf16), tail[:, :LAT]
        ) * (tail_part / total)
        for s in range(2):
            for b in range(LAT // 128):
                lat[b, pl.ds(s * 4 + i, heads, stride=8), :] = latent[
                    s * heads : (s + 1) * heads, b * 128 : (b + 1) * 128
                ]

    half = heads // 2
    per_chunk = half // CHUNKS
    load_uv.wait()

    def head_rows(h):
        return jnp.concatenate(
            [lat[b, h * 8 : (h + 1) * 8, :] for b in range(LAT // 128)], axis=1
        )

    def forward_heads(chunk):
        for step in range(1, Z_COUNT):
            other = z_at(step) * Y_COUNT + y
            arrived(hbuf.at[chunk, other], b_recv.at[chunk, other])
            send(
                hbuf.at[chunk, other],
                hbuf.at[chunk, other],
                b_send.at[chunk, 4 + step],
                b_recv.at[chunk, other],
                y_peer,
            )

    for chunk in range(CHUNKS):
        outs = []
        for p in range(per_chunk):
            h = chunk * per_chunk + p
            both = jnp.concatenate([head_rows(h), head_rows(h + half)], axis=0).astype(bf16)
            low_out = dot_f32(both, uv[h])[0:8]
            high_out = dot_f32(both, uv[h + half])[8:16]
            outs.append(jnp.concatenate([low_out, high_out], axis=0).astype(bf16))
        hbuf[chunk, d] = jnp.concatenate(outs, axis=1)
        for step in range(1, Z_COUNT):
            send(
                hbuf.at[chunk, d],
                hbuf.at[chunk, d],
                b_send.at[chunk, step],
                b_recv.at[chunk, d],
                (z_at(step) * Y_COUNT + y, t),
            )
        send(
            hbuf.at[chunk, d],
            hbuf.at[chunk, d],
            b_send.at[chunk, 0],
            b_recv.at[chunk, d],
            y_peer,
        )
        if chunk >= 1:
            forward_heads(chunk - 1)
    forward_heads(CHUNKS - 1)

    load_wo.wait()
    out_sum = None
    for chunk in range(CHUNKS):
        for step in range(Z_COUNT):
            other = z_at(step) * Y_COUNT + (1 - y)
            arrived(hbuf.at[chunk, other], b_recv.at[chunk, other])
        left = hbuf[chunk].reshape(dp_count * 16, per_chunk * 128)
        for a in range(2):
            first = a * half + chunk * per_chunk
            weight = wo[first : first + per_chunk].reshape(per_chunk * 128, block_width)
            product = dot_f32(left, weight).reshape(dp_count, 16, block_width)
            product = product[:, a * 8 : (a + 1) * 8, :]
            out_sum = product if out_sum is None else out_sum + product
    partial = []
    for s in range(2):
        tiles = []
        for k in range(dp_count):
            tiles.append(out_sum[k, s * 4 : s * 4 + 4])
        partial.append(jnp.concatenate(tiles, axis=0) + hidw[s])
    for xx in range(X_COUNT):
        for cc in range(CORES):
            piece = partial[cc][:, xx * 384 : xx * 384 + WINDOW]
            cpart[xx * CORES + cc] = piece
            csend[xx * CORES + cc] = piece.astype(bf16)
    for step in range(1, 4):
        other = lax.rem(t + step, 4)
        send(csend.at[other], crecv.at[t], c_send.at[step], c_recv.at[t], (d, other))
    gain = jnp.concatenate(
        [gain_v[pl.ds(d * (block_width // 128) + x * 3 + k, 1), :] for k in range(4)], axis=1
    )
    mixed = cpart[t]
    for step in range(1, 4):
        other = lax.rem(t + step, 4)
        arrived(crecv.at[other], c_recv.at[other])
        mixed = mixed + crecv[other].astype(f32)
    lanes = lax.broadcasted_iota(jnp.int32, mixed.shape, 1)
    pair = 2 * share
    mixed = jnp.where((lanes >= 64 * x) & (lanes < 64 * x + pair), mixed, 0.0)
    mixed_v[...] = mixed
    squares = jnp.sum(mixed * mixed, axis=1, keepdims=True)
    squares_high = squares.astype(bf16).astype(f32)
    spare = pair * (1 - x)
    own_block = mixed * gain
    own_block = jnp.where(lanes == spare, squares_high, own_block)
    own_block = jnp.where(lanes == spare + 1, squares - squares_high, own_block)

    def slot_of(xx, yy, zz):
        return (xx * Y_COUNT + yy) * Z_COUNT + zz

    own = slot_of(x, y, z)
    xbuf[own, c] = own_block.astype(bf16)

    def pass_on(slot, kind, number, device):
        send(
            xbuf.at[slot, c],
            xbuf.at[slot, c],
            d_send.at[kind, number],
            d_recv.at[slot * 2 + c],
            device,
        )

    for step in range(1, Z_COUNT):
        pass_on(own, 0, step, (z_at(step) * Y_COUNT + y, t))
    pass_on(own, 1, 0, y_peer)
    pass_on(own, 2, 0, x_peer)
    pass_on(own, 3, 0, core_peer)

    gacc[...] = jnp.zeros_like(gacc)
    uacc[...] = jnp.zeros_like(uacc)
    sqacc[...] = jnp.zeros_like(sqacc)
    load_wg.wait()
    load_wu.wait()
    block_lane = lax.broadcasted_iota(jnp.int32, (rows, WINDOW), 1)

    def use_block(xx, yy, zz):
        slot = slot_of(xx, yy, zz)
        arrived(xbuf.at[slot, 1 - c], d_recv.at[slot * 2 + (1 - c)])
        block = xbuf[slot].reshape(rows, WINDOW).astype(f32)
        inside = (block_lane >= 64 * xx) & (block_lane < 64 * xx + pair)
        block = jnp.where(inside, block, 0.0).astype(bf16)
        first = pl.multiple_of((zz * Y_COUNT + yy) * block_width + xx * 384, 128)
        gacc[...] += dot_rows(block, wg[:, pl.ds(first, WINDOW)])
        uacc[...] += dot_rows(block, wu[:, pl.ds(first, WINDOW)])
        lane = pl.multiple_of(384 * (1 - xx), 128)
        sqacc[xx] += xbuf[slot, :, :, pl.ds(lane, 128)].reshape(rows, 128).astype(f32)

    def take(xx, yy, zz):
        slot = slot_of(xx, yy, zz)
        arrived(xbuf.at[slot, c], d_recv.at[slot * 2 + c])
        return slot

    def from_z(m, carry):
        slot = take(x, y, z_at(m))
        pass_on(slot, 1, m, y_peer)
        pass_on(slot, 2, m, x_peer)
        pass_on(slot, 3, m, core_peer)
        return carry

    def from_sides(m):
        zz = z_at(m)
        odd = lax.rem(zz, 2)
        by_y = take(x, 1 - y, zz)

        @pl.when(odd == 0)
        def _():
            pass_on(by_y, 2, 4 + lax.div(zz, 2), x_peer)

        pass_on(by_y, 3, 4 + m, core_peer)
        by_x = take(1 - x, y, zz)

        @pl.when(odd == 1)
        def _():
            pass_on(by_x, 1, 4 + lax.div(zz, 2), y_peer)

        pass_on(by_x, 3, 8 + m, core_peer)

    def from_sides_and_use(m, carry):
        from_sides(m)
        use_block(x, y, z_at(m))
        return carry

    def from_corner_and_use(m, carry):
        zz = z_at(m)
        pass_on(take(1 - x, 1 - y, zz), 3, 12 + m, core_peer)
        use_block(x, 1 - y, zz)
        use_block(1 - x, y, zz)
        return carry

    def use_corner(m, carry):
        use_block(1 - x, 1 - y, z_at(m))
        return carry

    use_block(x, y, z)
    lax.fori_loop(1, Z_COUNT, from_z, 0)
    from_sides(jnp.int32(0))
    lax.fori_loop(1, Z_COUNT, from_sides_and_use, 0)
    lax.fori_loop(0, Z_COUNT, from_corner_and_use, 0)
    lax.fori_loop(0, Z_COUNT, use_corner, 0)

    sq_lane = lax.broadcasted_iota(jnp.int32, (rows, 128), 1)
    sq_all = jnp.where((sq_lane == pair - 384) | (sq_lane == pair - 383), sqacc[0], 0.0)
    sq_all = sq_all + jnp.where(sq_lane < 2, sqacc[1], 0.0)
    sq_total = jnp.sum(sq_all, axis=1, keepdims=True)
    token_scale = lax.rsqrt(sq_total / (block_width * dp_count) + norm_eps)
    gate = gacc[...] * token_scale
    by_token = gate / (1.0 + jnp.exp(-gate)) * (uacc[...] * token_scale)
    act[0:32] = jnp.where(c == 0, by_token[0:32], by_token[32:64]).astype(bf16)
    act[32:64] = jnp.where(c == 0, by_token[32:64], by_token[0:32]).astype(bf16)

    load_wd.wait()

    def dest_dp(i):
        yy = lax.rem(y + 1 + lax.div(i, Z_COUNT), 2)
        return z_at(1 + lax.rem(i, Z_COUNT)) * Y_COUNT + yy

    def first_turn(i):
        dd = dest_dp(i)
        zz = lax.div(dd, Y_COUNT)
        odd = lax.rem(zz, 2)
        arrived(e1r.at[dd], e1_recv.at[dd])

        def summed(xx):
            return keep1[dd, xx] + e1r[dd, xx].astype(f32)

        @pl.when(odd == 0)
        def _():
            e2s[dd] = summed(1 - x).astype(bf16)
            send(e2s.at[dd], e2r.at[dd], e2_send.at[dd], e2_recv.at[dd], x_peer)
            keep2[dd] = summed(x)

        @pl.when((odd == 1) & (i < Z_COUNT))
        def _():
            for xx in range(X_COUNT):
                k = zz * 2 + xx
                e2s[k] = summed(xx).astype(bf16)
                send(e2s.at[k], e2r.at[k], e2_send.at[k], e2_recv.at[k], y_peer)

        @pl.when((odd == 1) & (i >= Z_COUNT))
        def _():
            for xx in range(X_COUNT):
                keep2[zz * 2 + xx] = summed(xx)

    def down(i, carry):
        dd = dest_dp(i)
        first = pl.multiple_of(dd * block_width, 128)
        product = dot_f32(act[...], wd[:, pl.ds(first, block_width)])
        for xx in range(X_COUNT):
            window = slice(xx * 384, xx * 384 + WINDOW)
            keep1[dd, xx] = product[0:32, window]
            e1s[dd, xx] = product[32:64, window].astype(bf16)
        send(e1s.at[dd], e1r.at[dd], e1_send.at[dd], e1_recv.at[dd], core_peer)

        @pl.when(i >= 2)
        def _():
            first_turn(i - 2)

        return carry

    lax.fori_loop(0, dp_count, down, 0)
    first_turn(jnp.int32(dp_count - 2))
    first_turn(jnp.int32(dp_count - 1))
    for k in range(Z_COUNT):
        zz = z_at(1 + k)
        odd = lax.rem(zz, 2)
        sent_part = zz * 2 + (1 - y) + odd * (y - x)
        arrived(e2r.at[sent_part], e2_recv.at[sent_part])
        e3s[zz] = (keep2[sent_part] + e2r[sent_part].astype(f32)).astype(bf16)
        peer_y = y + (1 - odd) * (1 - 2 * y)
        peer_x = x + odd * (1 - 2 * x)
        send(
            e3s.at[zz],
            e3r.at[zz],
            e3_send.at[zz],
            e3_recv.at[zz],
            (z * Y_COUNT + peer_y, peer_x * CORES + c),
        )
    result = mixed_v[...]
    for k in range(Z_COUNT):
        zz = z_at(1 + k)
        dd = zz * Y_COUNT + y
        kept_part = zz * 2 + y + lax.rem(zz, 2) * (x - y)
        arrived(e2r.at[kept_part], e2_recv.at[kept_part])
        arrived(e3r.at[zz], e3_recv.at[zz])
        value = keep2[kept_part] + e2r[kept_part].astype(f32) + e3r[zz].astype(f32)
        if k < Z_COUNT - 1:
            e4s[zz] = value.astype(bf16)
            send(e4s.at[zz], e4r.at[z], e4_send.at[zz], e4_recv.at[z], (dd, t))
        else:
            result = result + value
    for step in range(1, Z_COUNT):
        other = z_at(step)
        arrived(e4r.at[other], e4_recv.at[other])
        result = result + e4r[other].astype(f32)
    halves = []
    for cc in range(CORES):
        near, far = cc * share, cc * share + 64
        shifted = pltpu.roll(result, WINDOW - far, 1)
        base = pltpu.roll(result, WINDOW - near, 1) if near else result
        halves.append(jnp.where(x == 0, base, shifted)[:, 0:256].astype(bf16))
    fsend[...] = jnp.where(c == 0, halves[1].astype(f32), halves[0].astype(f32)).astype(bf16)
    send(fsend, frecv, f_send.at[0], f_recv.at[0], core_peer)
    mine = jnp.where(c == 0, halves[0].astype(f32), halves[1].astype(f32)).astype(bf16)
    out_ref[c] = mine[:, 0:share]
    arrived(frecv, f_recv.at[0])
    out_ref[1 - c] = frecv[:, 0:share]

    for step in range(1, dp_count):
        sent(outg.at[own_rows(lax.rem(d + step, dp_count))], a_send.at[step])
    for chunk in range(CHUNKS):
        for number in range(8):
            if number != 4:
                sent(hbuf.at[chunk, d], b_send.at[chunk, number])
    for step in range(1, 4):
        sent(csend.at[lax.rem(t + step, 4)], c_send.at[step])
    for kind, numbers in ((0, range(1, 4)), (1, range(6)), (2, range(6)), (3, range(16))):
        for number in numbers:
            sent(xbuf.at[own, c], d_send.at[kind, number])
    for dd in range(dp_count):
        sent(e1s.at[dd], e1_send.at[dd])
        sent(e2s.at[dd], e2_send.at[dd])
    for zz in range(Z_COUNT):
        sent(e3s.at[zz], e3_send.at[zz])
    for step in range(1, Z_COUNT):
        sent(e4s.at[z_at(step)], e4_send.at[z_at(step)])
    sent(fsend, f_send.at[0])


def fused_shards(
    prefill_latent,
    request_slot,
    new_lengths,
    ctx_lengths,
    kv_cache,
    queries,
    step_latents,
    w_uv,
    w_out,
    hidden,
    ffn_gain,
    w_gate,
    w_up,
    w_down,
):
    f32, bf16 = jnp.float32, jnp.bfloat16
    width = queries.shape[3]
    heads = queries.shape[2]
    ff_share = w_down.shape[0]
    prefill_latent = prefill_latent.T
    new_lengths = new_lengths.T
    kv_cache = kv_cache.transpose(0, 2, 1)
    w_gate = w_gate.T
    w_up = w_up.T
    gain = ffn_gain.reshape(-1, 128)
    smem = pl.BlockSpec(memory_space=pltpu.SMEM)
    vmem = pl.BlockSpec(memory_space=pltpu.VMEM)
    hbm = pl.BlockSpec(memory_space=pl.ANY)
    dma = pltpu.SemaphoreType.DMA
    pieces = (32, WINDOW)
    scratch = [
        pltpu.VMEM(prefill_latent.shape, bf16),
        pltpu.VMEM(kv_cache.shape, bf16),
        pltpu.VMEM(queries.shape, bf16),
        pltpu.VMEM(step_latents.shape, bf16),
        pltpu.VMEM(w_uv.shape, bf16),
        pltpu.VMEM(w_out.shape, bf16),
        pltpu.VMEM(hidden.shape, bf16),
        pltpu.VMEM(w_gate.shape, bf16),
        pltpu.VMEM(w_up.shape, bf16),
        pltpu.VMEM(w_down.shape, bf16),
        pltpu.VMEM((prefill_latent.shape[1] + 128, width), bf16),
        pltpu.VMEM((prefill_latent.shape[1], width), bf16),
        pltpu.VMEM((4, 2 * heads, kv_cache.shape[2]), f32),
        pltpu.VMEM((LAT // 128, heads * 8, 128), f32),
        pltpu.VMEM((CHUNKS, 8, 16, heads // 2 // CHUNKS * 128), bf16),
        pltpu.VMEM((4, *pieces), f32),
        pltpu.VMEM((4, *pieces), bf16),
        pltpu.VMEM((4, *pieces), bf16),
        pltpu.VMEM((2, 32, w_out.shape[2]), f32),
        pltpu.VMEM(pieces, f32),
        pltpu.VMEM((16, 2, *pieces), bf16),
        pltpu.VMEM((64, ff_share), f32),
        pltpu.VMEM((64, ff_share), f32),
        pltpu.VMEM((2, 64, 128), f32),
        pltpu.VMEM((64, ff_share), bf16),
        pltpu.VMEM((8, 2, *pieces), bf16),
        pltpu.VMEM((8, 2, *pieces), bf16),
        pltpu.VMEM((8, 2, *pieces), f32),
        pltpu.VMEM((8, *pieces), bf16),
        pltpu.VMEM((8, *pieces), bf16),
        pltpu.VMEM((8, *pieces), f32),
        pltpu.VMEM((4, *pieces), bf16),
        pltpu.VMEM((4, *pieces), bf16),
        pltpu.VMEM((4, *pieces), bf16),
        pltpu.VMEM((4, *pieces), bf16),
        pltpu.VMEM((32, 256), bf16),
        pltpu.VMEM((32, 256), bf16),
        pltpu.VMEM((4, 2 * heads, LAT), f32),
        dma((16,)),
        dma((8,)),
        dma((8,)),
        dma((CHUNKS, 8)),
        dma((CHUNKS, 8)),
        dma((4,)),
        dma((4,)),
        dma((4, 16)),
        dma((32,)),
        dma((8,)),
        dma((8,)),
        dma((8,)),
        dma((8,)),
        dma((4,)),
        dma((4,)),
        dma((4,)),
        dma((4,)),
        dma((1,)),
        dma((1,)),
    ]
    return pl.pallas_call(
        layer_kernel,
        out_shape=jax.ShapeDtypeStruct(hidden.shape, bf16),
        in_specs=[smem] * 3 + [hbm] * 7 + [vmem] + [hbm] * 3,
        out_specs=vmem,
        scratch_shapes=scratch,
        compiler_params=pltpu.CompilerParams(
            collective_id=0, has_side_effects=True, vmem_limit_bytes=60 * 1024 * 1024
        ),
        cost_estimate=pl.CostEstimate(
            flops=4_000_000_000, bytes_accessed=42_000_000, transcendentals=400_000
        ),
    )(
        request_slot,
        new_lengths,
        ctx_lengths,
        prefill_latent,
        kv_cache,
        queries,
        step_latents,
        w_uv,
        w_out,
        hidden,
        gain,
        w_gate,
        w_up,
        w_down,
    )


def shards(dp_count, tp_count, *arrays):
    if (dp_count, tp_count) == (Z_COUNT * Y_COUNT, X_COUNT * CORES):
        return fused_shards(*arrays)
    return plain_shards(*arrays)


def solution(mesh):
    return jax.shard_map(
        functools.partial(shards, mesh.shape["dp"], mesh.shape["tp"]),
        mesh=mesh,
        in_specs=(
            P("dp", None),
            P(),
            P(),
            P("dp"),
            P("dp", None, None),
            P(None, "dp", "tp", None),
            P(None, "dp", None),
            P("tp", None, None),
            P("tp", None, "dp"),
            P(None, None, ("dp", "tp")),
            P(),
            P(None, ("dp", "tp")),
            P(None, ("dp", "tp")),
            P(("dp", "tp"), None),
        ),
        out_specs=P(None, None, ("dp", "tp")),
        check_vma=False,
    )
```

```python
import functools

import jax
import jax.numpy as jnp
from jax import lax
from jax.experimental import pallas as pl
from jax.experimental.pallas import tpu as pltpu
from jax.sharding import PartitionSpec as P

LAT = 512
QKD = 192
OWN_TOK = 16


masked_score = -1e30
norm_eps = 1e-06


def attend(query, step_ids, kv_cache, cache_mask, new_rows, new_mask, step_latents, w_uv):
    score_scale = QKD ** (-0.5)
    cache_scores = (
        jnp.einsum("sqhc,qkc->sqhk", query, kv_cache, preferred_element_type=jnp.float32)
        * score_scale
    )
    cache_scores = jnp.where(cache_mask[None, :, None, :], cache_scores, masked_score)
    fresh_scores = (
        jnp.einsum("sqhc,kc->sqhk", query, new_rows, preferred_element_type=jnp.float32)
        * score_scale
    )
    fresh_scores = jnp.where(new_mask[None, :, None, :], fresh_scores, masked_score)
    token_scores = (
        jnp.einsum("sqhc,tqc->sqht", query, step_latents, preferred_element_type=jnp.float32)
        * score_scale
    )
    token_valid = jnp.arange(step_latents.shape[0], dtype=jnp.int32)[None, :] <= step_ids[:, None]
    token_scores = jnp.where(token_valid[:, None, None, :], token_scores, masked_score)
    highest = jnp.maximum(
        jnp.maximum(jnp.max(cache_scores, axis=-1), jnp.max(fresh_scores, axis=-1)),
        jnp.max(token_scores, axis=-1),
    )[..., None]
    cache_exp = jnp.exp(cache_scores - highest)
    fresh_exp = jnp.exp(fresh_scores - highest)
    token_exp = jnp.exp(token_scores - highest)
    totals = (
        jnp.sum(cache_exp, axis=-1, keepdims=True)
        + jnp.sum(fresh_exp, axis=-1, keepdims=True)
        + jnp.sum(token_exp, axis=-1, keepdims=True)
    )
    cache_probs = (cache_exp / totals).astype(jnp.bfloat16)
    fresh_probs = (fresh_exp / totals).astype(jnp.bfloat16)
    token_probs = (token_exp / totals).astype(jnp.bfloat16)
    latent_out = jnp.einsum(
        "sqhk,qkc->sqhc", cache_probs, kv_cache[:, :, :LAT], preferred_element_type=jnp.float32
    )
    latent_out = latent_out + jnp.einsum(
        "sqhk,kc->sqhc", fresh_probs, new_rows[:, :LAT], preferred_element_type=jnp.float32
    )
    latent_out = latent_out + jnp.einsum(
        "sqht,tqc->sqhc", token_probs, step_latents[:, :, :LAT], preferred_element_type=jnp.float32
    )
    latent_out = latent_out.astype(jnp.bfloat16)
    return jnp.einsum(
        "sqhc,hcv->sqhv", latent_out, w_uv, preferred_element_type=jnp.float32
    ).astype(jnp.bfloat16)


def plain_shards(
    prefill_latent,
    request_slot,
    new_lengths,
    ctx_lengths,
    kv_cache,
    queries,
    step_latents,
    w_uv,
    w_out,
    hidden,
    ffn_gain,
    w_gate,
    w_up,
    w_down,
):
    dp_count = lax.axis_size("dp")
    dp_rank = lax.axis_index("dp")
    tp_rank = lax.axis_index("tp")
    per_owner = new_lengths.shape[1]
    total_requests = request_slot.shape[0]
    latent_width = kv_cache.shape[2]
    share_width = hidden.shape[2]
    block_width = w_out.shape[2]
    model_width = block_width * dp_count
    numbers = jnp.arange(total_requests, dtype=jnp.int32)
    one_hot = request_slot[:, None] == numbers[None, :]
    lengths_flat = new_lengths.reshape(-1)
    request_rows = jnp.sum(jnp.where(one_hot, lengths_flat[None, :], 0), axis=1)
    offsets = jnp.cumsum(request_rows) - request_rows
    inverse = jnp.sum(jnp.where(one_hot, numbers[:, None], 0), axis=0)
    slot_start = jnp.cumsum(new_lengths, axis=1) - new_lengths
    positions = jnp.arange(OWN_TOK, dtype=jnp.int32)
    slot_of_place = (
        jnp.sum((slot_start[:, :, None] <= positions[None, None, :]).astype(jnp.int32), axis=1) - 1
    )
    owner_ids = jnp.arange(dp_count, dtype=jnp.int32)[:, None]
    owner_rows = owner_ids * per_owner + slot_of_place
    start_in_slot = jnp.take_along_axis(slot_start, slot_of_place, axis=1)
    source_rows = (
        jnp.take(offsets, jnp.take(inverse, owner_rows)) + positions[None, :] - start_in_slot
    )
    outgoing = jnp.take(prefill_latent, source_rows.reshape(-1), axis=0).reshape(
        dp_count, OWN_TOK, latent_width
    )
    incoming = lax.all_to_all(outgoing, "dp", split_axis=0, concat_axis=0, tiled=True)
    new_rows = incoming.reshape(dp_count * OWN_TOK, latent_width)
    my_lengths = lax.dynamic_index_in_dim(new_lengths, dp_rank, 0, keepdims=False)
    my_start = jnp.cumsum(my_lengths) - my_lengths
    in_slot = (positions[None, :] >= my_start[:, None]) & (
        positions[None, :] < (my_start + my_lengths)[:, None]
    )
    new_mask = jnp.tile(in_slot, (1, dp_count))
    cache_mask = jnp.arange(kv_cache.shape[1], dtype=jnp.int32)[None, :] < ctx_lengths[:, None]
    share_first = tp_rank * share_width

    def finish(first, last):
        step_ids = jnp.arange(first, last, dtype=jnp.int32)
        steps_here = last - first
        head_out = attend(
            queries[first:last],
            step_ids,
            kv_cache,
            cache_mask,
            new_rows,
            new_mask,
            step_latents,
            w_uv,
        )
        every_row = lax.all_gather(head_out, "dp", axis=1, tiled=True)
        partial_value = jnp.dot(
            every_row.reshape(steps_here * total_requests, -1),
            w_out.reshape(-1, block_width),
            preferred_element_type=jnp.float32,
        )
        partial_value = partial_value.reshape(steps_here, total_requests, block_width)
        own_cols = lax.dynamic_slice_in_dim(partial_value, share_first, share_width, 2) + hidden[
            first:last
        ].astype(jnp.float32)
        partial_value = lax.dynamic_update_slice_in_dim(partial_value, own_cols, share_first, 2)
        mixed = lax.psum_scatter(partial_value, "tp", scatter_dimension=2, tiled=True)
        squares = lax.psum(jnp.sum(mixed * mixed, axis=-1), ("dp", "tp"))
        gain_part = lax.dynamic_slice_in_dim(
            ffn_gain, dp_rank * block_width + share_first, share_width
        )
        scaled_part = (mixed * gain_part).astype(jnp.bfloat16)
        scaled = lax.all_gather(scaled_part, ("dp", "tp"), axis=2, tiled=True)
        flat_input = scaled.reshape(steps_here * total_requests, model_width)
        row_scale = lax.rsqrt(squares / model_width + norm_eps).reshape(-1, 1)
        gate_out = jnp.dot(flat_input, w_gate, preferred_element_type=jnp.float32) * row_scale
        up_out = jnp.dot(flat_input, w_up, preferred_element_type=jnp.float32) * row_scale
        activated = (jax.nn.silu(gate_out) * up_out).astype(jnp.bfloat16)
        down_out = jnp.dot(activated, w_down, preferred_element_type=jnp.float32).reshape(
            steps_here, total_requests, model_width
        )
        ffn_part = lax.psum_scatter(down_out, ("dp", "tp"), scatter_dimension=2, tiled=True)
        return (mixed + ffn_part).astype(jnp.bfloat16)

    return finish(0, queries.shape[0])


Z_COUNT, Y_COUNT, X_COUNT, CORES = 4, 2, 2, 2
CHUNKS = 4
WINDOW = 512


def dot_f32(left, right):
    return jnp.dot(left, right, preferred_element_type=jnp.float32)


def dot_rows(left, right):
    return lax.dot_general(
        left, right, (((1,), (1,)), ((), ())), preferred_element_type=jnp.float32
    )


def layer_kernel(
    slot_s,
    len_s,
    ctx_s,
    pre_h,
    kv_h,
    qry_h,
    stp_h,
    uv_h,
    wo_h,
    hid_h,
    gain_v,
    wg_h,
    wu_h,
    wd_h,
    out_ref,
    pre,
    kv,
    qry,
    stp,
    uv,
    wo,
    hid,
    wg,
    wu,
    wd,
    tail,
    outg,
    score,
    lat,
    hbuf,
    cpart,
    csend,
    crecv,
    hidw,
    mixed_v,
    xbuf,
    gacc,
    uacc,
    sqacc,
    act,
    e1s,
    e1r,
    keep1,
    e2s,
    e2r,
    keep2,
    e3s,
    e3r,
    e4s,
    e4r,
    fsend,
    frecv,
    cache_out,
    load_sem,
    a_send,
    a_recv,
    b_send,
    b_recv,
    c_send,
    c_recv,
    d_send,
    d_recv,
    e1_send,
    e1_recv,
    e2_send,
    e2_recv,
    e3_send,
    e3_recv,
    e4_send,
    e4_recv,
    f_send,
    f_recv,
):
    f32, bf16 = jnp.float32, jnp.bfloat16
    dp_count = Z_COUNT * Y_COUNT
    d = lax.axis_index("dp")
    t = lax.axis_index("tp")
    z, y = lax.div(d, Y_COUNT), lax.rem(d, Y_COUNT)
    x, c = lax.div(t, CORES), lax.rem(t, CORES)
    heads = qry.shape[2]
    share = hid.shape[2]
    block_width = 4 * share
    rows = 2 * 4 * dp_count
    y_peer = (z * Y_COUNT + (1 - y), t)
    x_peer = (d, (1 - x) * CORES + c)
    core_peer = (d, x * CORES + (1 - c))

    def z_at(step):
        low = lax.rem(z + step, 2)
        high = lax.rem(lax.div(z, 2) + lax.div(jnp.int32(step), 2), 2)
        return high * 2 + low

    def send(src, dst, send_sem, recv_sem, device):
        copy = pltpu.make_async_remote_copy(
            src_ref=src,
            dst_ref=dst,
            send_sem=send_sem,
            recv_sem=recv_sem,
            device_id=device,
            device_id_type=pl.DeviceIdType.MESH,
        )
        copy.start()

    def arrived(ref, sem):
        pltpu.make_async_remote_copy(
            src_ref=ref,
            dst_ref=ref,
            send_sem=sem,
            recv_sem=sem,
            device_id=y_peer,
            device_id_type=pl.DeviceIdType.MESH,
        ).wait_recv()

    def sent(ref, sem):
        pltpu.make_async_remote_copy(
            src_ref=ref,
            dst_ref=ref,
            send_sem=sem,
            recv_sem=sem,
            device_id=y_peer,
            device_id_type=pl.DeviceIdType.MESH,
        ).wait_send()

    barrier = pltpu.get_barrier_semaphore()
    for step in range(1, dp_count):
        pl.semaphore_signal(
            barrier,
            inc=1,
            device_id=(lax.rem(d + step, dp_count), t),
            device_id_type=pl.DeviceIdType.MESH,
        )
    for step in range(1, 4):
        pl.semaphore_signal(
            barrier,
            inc=1,
            device_id=(d, lax.rem(t + step, 4)),
            device_id_type=pl.DeviceIdType.MESH,
        )

    def load(index, src, dst):
        copy = pltpu.make_async_copy(src, dst, load_sem.at[index])
        copy.start()
        return copy

    load_pre = load(0, pre_h, pre)
    load_stp = load(1, stp_h, stp)
    load_qry = load(2, qry_h, qry)
    load_kv = [load(3 + i, kv_h.at[i], kv.at[i]) for i in range(4)]
    load_hid = load(7, hid_h, hid)
    load_uv = load(8, uv_h, uv)

    pf_rows = pre.shape[1]
    source = lax.broadcasted_iota(jnp.int32, (8, pf_rows), 1)

    def place_request(r, carry):
        dest, offset = carry
        owner_row = slot_s[r]
        owner = lax.shift_right_logical(owner_row, 2)
        place = owner_row & 3
        count = len_s[place, owner]
        start = jnp.int32(0)
        for k in range(3):
            start = start + jnp.where(place > k, len_s[k, owner], 0)
        inside = (source >= offset) & (source < offset + count)
        dest = jnp.where(inside, source + (owner * OWN_TOK + start - offset), dest)
        return dest, offset + count

    dest, _ = lax.fori_loop(
        0, 4 * dp_count, place_request, (jnp.full((8, pf_rows), -1, jnp.int32), jnp.int32(0))
    )
    target = lax.broadcasted_iota(jnp.int32, (pf_rows, pf_rows), 0)
    pick = jnp.where(target == dest[0:1], 1.0, 0.0).astype(bf16)
    load_pre.wait()
    outg[...] = dot_rows(pick, pre[...]).astype(bf16)
    pl.semaphore_wait(barrier, dp_count - 1 + 3)

    def own_rows(index):
        return pl.ds(pl.multiple_of(index * OWN_TOK, OWN_TOK), OWN_TOK)

    for step in range(1, dp_count):
        other = lax.rem(d + step, dp_count)
        send(
            outg.at[own_rows(other)],
            tail.at[own_rows(d)],
            a_send.at[step],
            a_recv.at[d],
            (other, t),
        )
    tail[own_rows(d), :] = outg[own_rows(d), :]
    load_stp.wait()
    tokens = jnp.concatenate(
        [
            stp[0].astype(f32),
            stp[1].astype(f32),
            jnp.zeros((tail.shape[0] - pf_rows - 8, stp.shape[2]), f32),
        ],
        axis=0,
    )
    tail[pf_rows:, :] = tokens.astype(bf16)

    load_qry.wait()
    key_block = 256
    for i in range(4):
        load_kv[i].wait()
        query = jnp.concatenate([qry[0, i], qry[1, i]], axis=0)
        for k in range(kv.shape[2] // key_block):
            part = slice(k * key_block, (k + 1) * key_block)
            score[i, :, part] = dot_f32(query, kv[i, :, part])
        if i == 1:
            load_wo = load(9, wo_h, wo)
    load_wg = load(10, wg_h, wg)
    load_wu = load(11, wu_h, wu)
    load_wd = load(12, wd_h, wd)

    load_hid.wait()
    hidw[...] = jnp.zeros_like(hidw)
    for s in range(2):
        hidw[s, :, 0:share] = hid[s].astype(f32)
    for s in range(2):
        narrow = hidw[s]
        placed = narrow
        for k in range(1, 4):
            placed = jnp.where(t == k, pltpu.roll(narrow, k * share, 1), placed)
        hidw[s] = placed

    scale = QKD ** (-0.5)
    q_rows = 2 * heads
    key_col = lax.broadcasted_iota(jnp.int32, (q_rows, kv.shape[2]), 1)
    cache_max, cache_sum = [], []
    for i in range(4):
        cache_score = jnp.where(key_col < ctx_s[i], score[i] * scale, masked_score)
        top = jnp.max(cache_score, axis=1, keepdims=True)
        cache_exp = jnp.exp(cache_score - top)
        cache_max.append(top)
        cache_sum.append(jnp.sum(cache_exp, axis=1, keepdims=True))
        cache_out[i] = jnp.transpose(dot_rows(kv[i, 0:LAT, :], cache_exp.astype(bf16)))

    for step in range(1, dp_count):
        other = lax.rem(d + step, dp_count)
        arrived(tail.at[own_rows(other)], a_recv.at[other])

    tail_col = lax.broadcasted_iota(jnp.int32, (q_rows, tail.shape[0]), 1)
    tail_step = lax.broadcasted_iota(jnp.int32, (q_rows, tail.shape[0]), 0) // heads
    spot = tail_col & (OWN_TOK - 1)
    token = tail_col - pf_rows
    token_place = token & 3
    token_ok = (token >= 0) & (token < 8) & (lax.shift_right_arithmetic(token, 2) <= tail_step)
    start = jnp.int32(0)
    for i in range(4):
        count = len_s[i, d]
        query = jnp.concatenate([qry[0, i], qry[1, i]], axis=0)
        tail_score = dot_rows(query, tail[...]) * scale
        fresh_ok = (tail_col < pf_rows) & (spot >= start) & (spot < start + count)
        start = start + count
        tail_score = jnp.where(
            fresh_ok | (token_ok & (token_place == i)), tail_score, masked_score
        )
        tail_max = jnp.max(tail_score, axis=1, keepdims=True)
        tail_exp = jnp.exp(tail_score - tail_max)
        tail_sum = jnp.sum(tail_exp, axis=1, keepdims=True)
        highest = jnp.maximum(cache_max[i], tail_max)
        cache_part = jnp.exp(cache_max[i] - highest)
        tail_part = jnp.exp(tail_max - highest)
        total = cache_sum[i] * cache_part + tail_sum * tail_part
        latent = cache_out[i] * (cache_part / total) + dot_f32(
            tail_exp.astype(bf16), tail[:, :LAT]
        ) * (tail_part / total)
        for s in range(2):
            for b in range(LAT // 128):
                lat[b, pl.ds(s * 4 + i, heads, stride=8), :] = latent[
                    s * heads : (s + 1) * heads, b * 128 : (b + 1) * 128
                ]

    half = heads // 2
    per_chunk = half // CHUNKS
    load_uv.wait()

    def head_rows(h):
        return jnp.concatenate(
            [lat[b, h * 8 : (h + 1) * 8, :] for b in range(LAT // 128)], axis=1
        )

    def forward_heads(chunk):
        for step in range(1, Z_COUNT):
            other = z_at(step) * Y_COUNT + y
            arrived(hbuf.at[chunk, other], b_recv.at[chunk, other])
            send(
                hbuf.at[chunk, other],
                hbuf.at[chunk, other],
                b_send.at[chunk, 4 + step],
                b_recv.at[chunk, other],
                y_peer,
            )

    for chunk in range(CHUNKS):
        outs = []
        for p in range(per_chunk):
            h = chunk * per_chunk + p
            both = jnp.concatenate([head_rows(h), head_rows(h + half)], axis=0).astype(bf16)
            low_out = dot_f32(both, uv[h])[0:8]
            high_out = dot_f32(both, uv[h + half])[8:16]
            outs.append(jnp.concatenate([low_out, high_out], axis=0).astype(bf16))
        hbuf[chunk, d] = jnp.concatenate(outs, axis=1)
        for step in range(1, Z_COUNT):
            send(
                hbuf.at[chunk, d],
                hbuf.at[chunk, d],
                b_send.at[chunk, step],
                b_recv.at[chunk, d],
                (z_at(step) * Y_COUNT + y, t),
            )
        send(
            hbuf.at[chunk, d],
            hbuf.at[chunk, d],
            b_send.at[chunk, 0],
            b_recv.at[chunk, d],
            y_peer,
        )
        if chunk >= 1:
            forward_heads(chunk - 1)
    forward_heads(CHUNKS - 1)

    load_wo.wait()
    out_sum = None
    for chunk in range(CHUNKS):
        for step in range(Z_COUNT):
            other = z_at(step) * Y_COUNT + (1 - y)
            arrived(hbuf.at[chunk, other], b_recv.at[chunk, other])
        left = hbuf[chunk].reshape(dp_count * 16, per_chunk * 128)
        for a in range(2):
            first = a * half + chunk * per_chunk
            weight = wo[first : first + per_chunk].reshape(per_chunk * 128, block_width)
            product = dot_f32(left, weight).reshape(dp_count, 16, block_width)
            product = product[:, a * 8 : (a + 1) * 8, :]
            out_sum = product if out_sum is None else out_sum + product
    partial = []
    for s in range(2):
        tiles = []
        for k in range(dp_count):
            tiles.append(out_sum[k, s * 4 : s * 4 + 4])
        partial.append(jnp.concatenate(tiles, axis=0) + hidw[s])
    for xx in range(X_COUNT):
        for cc in range(CORES):
            piece = partial[cc][:, xx * 384 : xx * 384 + WINDOW]
            cpart[xx * CORES + cc] = piece
            csend[xx * CORES + cc] = piece.astype(bf16)
    for step in range(1, 4):
        other = lax.rem(t + step, 4)
        send(csend.at[other], crecv.at[t], c_send.at[step], c_recv.at[t], (d, other))
    gain = jnp.concatenate(
        [gain_v[pl.ds(d * (block_width // 128) + x * 3 + k, 1), :] for k in range(4)], axis=1
    )
    mixed = cpart[t]
    for step in range(1, 4):
        other = lax.rem(t + step, 4)
        arrived(crecv.at[other], c_recv.at[other])
        mixed = mixed + crecv[other].astype(f32)
    lanes = lax.broadcasted_iota(jnp.int32, mixed.shape, 1)
    pair = 2 * share
    mixed = jnp.where((lanes >= 64 * x) & (lanes < 64 * x + pair), mixed, 0.0)
    mixed_v[...] = mixed
    squares = jnp.sum(mixed * mixed, axis=1, keepdims=True)
    squares_high = squares.astype(bf16).astype(f32)
    spare = pair * (1 - x)
    own_block = mixed * gain
    own_block = jnp.where(lanes == spare, squares_high, own_block)
    own_block = jnp.where(lanes == spare + 1, squares - squares_high, own_block)

    def slot_of(xx, yy, zz):
        return (xx * Y_COUNT + yy) * Z_COUNT + zz

    own = slot_of(x, y, z)
    xbuf[own, c] = own_block.astype(bf16)

    def pass_on(slot, kind, number, device):
        send(
            xbuf.at[slot, c],
            xbuf.at[slot, c],
            d_send.at[kind, number],
            d_recv.at[slot * 2 + c],
            device,
        )

    for step in range(1, Z_COUNT):
        pass_on(own, 0, step, (z_at(step) * Y_COUNT + y, t))
    pass_on(own, 1, 0, y_peer)
    pass_on(own, 2, 0, x_peer)
    pass_on(own, 3, 0, core_peer)

    gacc[...] = jnp.zeros_like(gacc)
    uacc[...] = jnp.zeros_like(uacc)
    sqacc[...] = jnp.zeros_like(sqacc)
    load_wg.wait()
    load_wu.wait()
    block_lane = lax.broadcasted_iota(jnp.int32, (rows, WINDOW), 1)

    def use_block(xx, yy, zz):
        slot = slot_of(xx, yy, zz)
        arrived(xbuf.at[slot, 1 - c], d_recv.at[slot * 2 + (1 - c)])
        block = xbuf[slot].reshape(rows, WINDOW).astype(f32)
        inside = (block_lane >= 64 * xx) & (block_lane < 64 * xx + pair)
        block = jnp.where(inside, block, 0.0).astype(bf16)
        first = pl.multiple_of((zz * Y_COUNT + yy) * block_width + xx * 384, 128)
        gacc[...] += dot_rows(wg[:, pl.ds(first, WINDOW)], block)
        uacc[...] += dot_rows(wu[:, pl.ds(first, WINDOW)], block)
        lane = pl.multiple_of(384 * (1 - xx), 128)
        sqacc[xx] += xbuf[slot, :, :, pl.ds(lane, 128)].reshape(rows, 128).astype(f32)

    def take(xx, yy, zz):
        slot = slot_of(xx, yy, zz)
        arrived(xbuf.at[slot, c], d_recv.at[slot * 2 + c])
        return slot

    def from_z(m, carry):
        slot = take(x, y, z_at(m))
        pass_on(slot, 1, m, y_peer)
        pass_on(slot, 2, m, x_peer)
        pass_on(slot, 3, m, core_peer)
        return carry

    def from_sides(m):
        zz = z_at(m)
        odd = lax.rem(zz, 2)
        by_y = take(x, 1 - y, zz)

        @pl.when(odd == 0)
        def _():
            pass_on(by_y, 2, 4 + lax.div(zz, 2), x_peer)

        pass_on(by_y, 3, 4 + m, core_peer)
        by_x = take(1 - x, y, zz)

        @pl.when(odd == 1)
        def _():
            pass_on(by_x, 1, 4 + lax.div(zz, 2), y_peer)

        pass_on(by_x, 3, 8 + m, core_peer)

    def from_sides_and_use(m, carry):
        from_sides(m)
        use_block(x, y, z_at(m))
        return carry

    def from_corner_and_use(m, carry):
        zz = z_at(m)
        use_block(x, 1 - y, zz)
        pass_on(take(1 - x, 1 - y, zz), 3, 12 + m, core_peer)
        use_block(1 - x, y, zz)
        return carry

    def use_corner(m, carry):
        use_block(1 - x, 1 - y, z_at(m))
        return carry

    lax.fori_loop(1, 3, from_z, 0)
    use_block(x, y, z)
    from_z(jnp.int32(3), 0)
    from_sides(jnp.int32(0))
    lax.fori_loop(1, Z_COUNT, from_sides_and_use, 0)
    lax.fori_loop(0, Z_COUNT, from_corner_and_use, 0)
    lax.fori_loop(0, Z_COUNT, use_corner, 0)

    sq_lane = lax.broadcasted_iota(jnp.int32, (rows, 128), 1)
    sq_all = jnp.where((sq_lane == pair - 384) | (sq_lane == pair - 383), sqacc[0], 0.0)
    sq_all = sq_all + jnp.where(sq_lane < 2, sqacc[1], 0.0)
    sq_total = jnp.sum(jnp.transpose(sq_all), axis=0, keepdims=True)
    token_scale = lax.rsqrt(sq_total / (block_width * dp_count) + norm_eps)
    gate = gacc[...] * token_scale
    hidden_units = gate / (1.0 + jnp.exp(-gate)) * (uacc[...] * token_scale)
    by_token = jnp.transpose(hidden_units)
    act[0:32] = jnp.where(c == 0, by_token[0:32], by_token[32:64]).astype(bf16)
    act[32:64] = jnp.where(c == 0, by_token[32:64], by_token[0:32]).astype(bf16)

    load_wd.wait()

    def dest_dp(i):
        yy = lax.rem(y + 1 + lax.div(i, Z_COUNT), 2)
        return z_at(1 + lax.rem(i, Z_COUNT)) * Y_COUNT + yy

    def first_turn(i):
        dd = dest_dp(i)
        zz = lax.div(dd, Y_COUNT)
        odd = lax.rem(zz, 2)
        arrived(e1r.at[dd], e1_recv.at[dd])

        def summed(xx):
            return keep1[dd, xx] + e1r[dd, xx].astype(f32)

        @pl.when(odd == 0)
        def _():
            e2s[dd] = summed(1 - x).astype(bf16)
            send(e2s.at[dd], e2r.at[dd], e2_send.at[dd], e2_recv.at[dd], x_peer)
            keep2[dd] = summed(x)

        @pl.when((odd == 1) & (i < Z_COUNT))
        def _():
            for xx in range(X_COUNT):
                k = zz * 2 + xx
                e2s[k] = summed(xx).astype(bf16)
                send(e2s.at[k], e2r.at[k], e2_send.at[k], e2_recv.at[k], y_peer)

        @pl.when((odd == 1) & (i >= Z_COUNT))
        def _():
            for xx in range(X_COUNT):
                keep2[zz * 2 + xx] = summed(xx)

    def down(i, carry):
        dd = dest_dp(i)
        first = pl.multiple_of(dd * block_width, 128)
        product = dot_f32(act[...], wd[:, pl.ds(first, block_width)])
        for xx in range(X_COUNT):
            window = slice(xx * 384, xx * 384 + WINDOW)
            keep1[dd, xx] = product[0:32, window]
            e1s[dd, xx] = product[32:64, window].astype(bf16)
        send(e1s.at[dd], e1r.at[dd], e1_send.at[dd], e1_recv.at[dd], core_peer)

        @pl.when(i >= 2)
        def _():
            first_turn(i - 2)

        return carry

    lax.fori_loop(0, dp_count, down, 0)
    first_turn(jnp.int32(dp_count - 2))
    first_turn(jnp.int32(dp_count - 1))
    for k in range(Z_COUNT):
        zz = z_at(1 + k)
        odd = lax.rem(zz, 2)
        sent_part = zz * 2 + (1 - y) + odd * (y - x)
        arrived(e2r.at[sent_part], e2_recv.at[sent_part])
        e3s[zz] = (keep2[sent_part] + e2r[sent_part].astype(f32)).astype(bf16)
        peer_y = y + (1 - odd) * (1 - 2 * y)
        peer_x = x + odd * (1 - 2 * x)
        send(
            e3s.at[zz],
            e3r.at[zz],
            e3_send.at[zz],
            e3_recv.at[zz],
            (z * Y_COUNT + peer_y, peer_x * CORES + c),
        )
    result = mixed_v[...]
    for k in range(Z_COUNT):
        zz = z_at(1 + k)
        dd = zz * Y_COUNT + y
        kept_part = zz * 2 + y + lax.rem(zz, 2) * (x - y)
        arrived(e2r.at[kept_part], e2_recv.at[kept_part])
        arrived(e3r.at[zz], e3_recv.at[zz])
        value = keep2[kept_part] + e2r[kept_part].astype(f32) + e3r[zz].astype(f32)
        if k < Z_COUNT - 1:
            e4s[zz] = value.astype(bf16)
            send(e4s.at[zz], e4r.at[z], e4_send.at[zz], e4_recv.at[z], (dd, t))
        else:
            result = result + value
    for step in range(1, Z_COUNT):
        other = z_at(step)
        arrived(e4r.at[other], e4_recv.at[other])
        result = result + e4r[other].astype(f32)
    halves = []
    for cc in range(CORES):
        near, far = cc * share, cc * share + 64
        shifted = pltpu.roll(result, WINDOW - far, 1)
        base = pltpu.roll(result, WINDOW - near, 1) if near else result
        halves.append(jnp.where(x == 0, base, shifted)[:, 0:256].astype(bf16))
    fsend[...] = jnp.where(c == 0, halves[1].astype(f32), halves[0].astype(f32)).astype(bf16)
    send(fsend, frecv, f_send.at[0], f_recv.at[0], core_peer)
    mine = jnp.where(c == 0, halves[0].astype(f32), halves[1].astype(f32)).astype(bf16)
    out_ref[c] = mine[:, 0:share]
    arrived(frecv, f_recv.at[0])
    out_ref[1 - c] = frecv[:, 0:share]

    for step in range(1, dp_count):
        sent(outg.at[own_rows(lax.rem(d + step, dp_count))], a_send.at[step])
    for chunk in range(CHUNKS):
        for number in range(8):
            if number != 4:
                sent(hbuf.at[chunk, d], b_send.at[chunk, number])
    for step in range(1, 4):
        sent(csend.at[lax.rem(t + step, 4)], c_send.at[step])
    for kind, numbers in ((0, range(1, 4)), (1, range(6)), (2, range(6)), (3, range(16))):
        for number in numbers:
            sent(xbuf.at[own, c], d_send.at[kind, number])
    for dd in range(dp_count):
        sent(e1s.at[dd], e1_send.at[dd])
        sent(e2s.at[dd], e2_send.at[dd])
    for zz in range(Z_COUNT):
        sent(e3s.at[zz], e3_send.at[zz])
    for step in range(1, Z_COUNT):
        sent(e4s.at[z_at(step)], e4_send.at[z_at(step)])
    sent(fsend, f_send.at[0])


def fused_shards(
    prefill_latent,
    request_slot,
    new_lengths,
    ctx_lengths,
    kv_cache,
    queries,
    step_latents,
    w_uv,
    w_out,
    hidden,
    ffn_gain,
    w_gate,
    w_up,
    w_down,
):
    f32, bf16 = jnp.float32, jnp.bfloat16
    width = queries.shape[3]
    heads = queries.shape[2]
    ff_share = w_down.shape[0]
    prefill_latent = prefill_latent.T
    new_lengths = new_lengths.T
    kv_cache = kv_cache.transpose(0, 2, 1)
    w_gate = w_gate.T
    w_up = w_up.T
    gain = ffn_gain.reshape(-1, 128)
    smem = pl.BlockSpec(memory_space=pltpu.SMEM)
    vmem = pl.BlockSpec(memory_space=pltpu.VMEM)
    hbm = pl.BlockSpec(memory_space=pl.ANY)
    dma = pltpu.SemaphoreType.DMA
    pieces = (32, WINDOW)
    scratch = [
        pltpu.VMEM(prefill_latent.shape, bf16),
        pltpu.VMEM(kv_cache.shape, bf16),
        pltpu.VMEM(queries.shape, bf16),
        pltpu.VMEM(step_latents.shape, bf16),
        pltpu.VMEM(w_uv.shape, bf16),
        pltpu.VMEM(w_out.shape, bf16),
        pltpu.VMEM(hidden.shape, bf16),
        pltpu.VMEM(w_gate.shape, bf16),
        pltpu.VMEM(w_up.shape, bf16),
        pltpu.VMEM(w_down.shape, bf16),
        pltpu.VMEM((prefill_latent.shape[1] + 128, width), bf16),
        pltpu.VMEM((prefill_latent.shape[1], width), bf16),
        pltpu.VMEM((4, 2 * heads, kv_cache.shape[2]), f32),
        pltpu.VMEM((LAT // 128, heads * 8, 128), f32),
        pltpu.VMEM((CHUNKS, 8, 16, heads // 2 // CHUNKS * 128), bf16),
        pltpu.VMEM((4, *pieces), f32),
        pltpu.VMEM((4, *pieces), bf16),
        pltpu.VMEM((4, *pieces), bf16),
        pltpu.VMEM((2, 32, w_out.shape[2]), f32),
        pltpu.VMEM(pieces, f32),
        pltpu.VMEM((16, 2, *pieces), bf16),
        pltpu.VMEM((ff_share, 64), f32),
        pltpu.VMEM((ff_share, 64), f32),
        pltpu.VMEM((2, 64, 128), f32),
        pltpu.VMEM((64, ff_share), bf16),
        pltpu.VMEM((8, 2, *pieces), bf16),
        pltpu.VMEM((8, 2, *pieces), bf16),
        pltpu.VMEM((8, 2, *pieces), f32),
        pltpu.VMEM((8, *pieces), bf16),
        pltpu.VMEM((8, *pieces), bf16),
        pltpu.VMEM((8, *pieces), f32),
        pltpu.VMEM((4, *pieces), bf16),
        pltpu.VMEM((4, *pieces), bf16),
        pltpu.VMEM((4, *pieces), bf16),
        pltpu.VMEM((4, *pieces), bf16),
        pltpu.VMEM((32, 256), bf16),
        pltpu.VMEM((32, 256), bf16),
        pltpu.VMEM((4, 2 * heads, LAT), f32),
        dma((16,)),
        dma((8,)),
        dma((8,)),
        dma((CHUNKS, 8)),
        dma((CHUNKS, 8)),
        dma((4,)),
        dma((4,)),
        dma((4, 16)),
        dma((32,)),
        dma((8,)),
        dma((8,)),
        dma((8,)),
        dma((8,)),
        dma((4,)),
        dma((4,)),
        dma((4,)),
        dma((4,)),
        dma((1,)),
        dma((1,)),
    ]
    return pl.pallas_call(
        layer_kernel,
        out_shape=jax.ShapeDtypeStruct(hidden.shape, bf16),
        in_specs=[smem] * 3 + [hbm] * 7 + [vmem] + [hbm] * 3,
        out_specs=vmem,
        scratch_shapes=scratch,
        compiler_params=pltpu.CompilerParams(
            collective_id=0, has_side_effects=True, vmem_limit_bytes=60 * 1024 * 1024
        ),
        cost_estimate=pl.CostEstimate(
            flops=4_000_000_000, bytes_accessed=42_000_000, transcendentals=400_000
        ),
    )(
        request_slot,
        new_lengths,
        ctx_lengths,
        prefill_latent,
        kv_cache,
        queries,
        step_latents,
        w_uv,
        w_out,
        hidden,
        gain,
        w_gate,
        w_up,
        w_down,
    )


def shards(dp_count, tp_count, *arrays):
    if (dp_count, tp_count) == (Z_COUNT * Y_COUNT, X_COUNT * CORES):
        return fused_shards(*arrays)
    return plain_shards(*arrays)


def solution(mesh):
    return jax.shard_map(
        functools.partial(shards, mesh.shape["dp"], mesh.shape["tp"]),
        mesh=mesh,
        in_specs=(
            P("dp", None),
            P(),
            P(),
            P("dp"),
            P("dp", None, None),
            P(None, "dp", "tp", None),
            P(None, "dp", None),
            P("tp", None, None),
            P("tp", None, "dp"),
            P(None, None, ("dp", "tp")),
            P(),
            P(None, ("dp", "tp")),
            P(None, ("dp", "tp")),
            P(("dp", "tp"), None),
        ),
        out_specs=P(None, None, ("dp", "tp")),
        check_vma=False,
    )
```
